512 devices in a mesh: ctx: 16 (over z_lo, y), head: 32 (over z_hi, x, core).
Axes of the slice: x: 4, y: 4, z: 16 (z_hi: 4, z_lo: 4; z = z_hi * 4 + z_lo), core: 2. Of those that a mesh axis runs over, the one named last changes fastest.
Arguments:
- inputs: bfloat16 [2048, 8192], P('head', 'ctx'), may hold values from -6 to 6
- queries: bfloat16 [2048, 8192], P('ctx', 'head'), may hold values from -140 to 140
- keys: bfloat16 [2048, 1024], P('ctx'), may hold values from -6 to 6
- values: bfloat16 [2048, 1024], P('ctx'), may hold values from -6 to 6
- outputs: bfloat16 [2048, 8192], P('ctx', 'head'), may hold values from -0.59765625 to 0.59765625
- out_grad: bfloat16 [2048, 8192], P('ctx', 'head'), may hold values from -6 to 6
- block_mask: int32 [32, 32], replicated, may hold values from 0 to 1, as said below
Outputs:
- q_grad: bfloat16 [2048, 8192], P('ctx', 'head')
- kv_grad: bfloat16 [2048, 2048], P('ctx', 'head')
- weight_q_grad: bfloat16 [8192, 8192], P('ctx', 'head')
- weight_kv_grad: bfloat16 [8192, 2048], P('ctx', 'head')
The draws below stay inside these ranges and needn't reach their ends.
Inputs may be any that keep to these rules, and one draw needn't show every extreme that they name: block_mask is 1 on its diagonal and 0 above it; below it entries are 0 or 1.
All inputs are finite; a program needn't handle non-finite values.
Results may differ from the reference program's by a relative error of at most 0.022.
Values may be sent and summed in bfloat16 or wider, within the bound.
A program may use at most 64 MiB of HBM per device.

```python
import jax
import jax.numpy as jnp
from jax import lax

D = 8192
HQ = 64
KVH = 8
HD = 128
BLK = 64
TOKENS = 2048
N_HEAD = 32


def shared_keys(key):
    base = jax.random.normal(key, (TOKENS, KVH * HD), jnp.float32)
    return jnp.clip(base, -6.0, 6.0)


def draw_keys(key, part):
    base = shared_keys(key)
    return base.astype(jnp.bfloat16)


def draw_queries(key, part):
    key = jax.random.fold_in(key, 7)
    first_key = jax.random.fold_in(key, 0)
    result = jnp.clip(jax.random.normal(first_key, (TOKENS, HQ * HD), jnp.float32), -6.0, 6.0)
    return result.astype(jnp.bfloat16)


def draw_block_mask(key, part):
    key = jax.random.fold_in(key, 3)
    first_key, second_key = jax.random.split(key)
    block_count = TOKENS // BLK
    levels = jax.random.randint(first_key, (block_count, 1), 1, 5)
    coins = jax.random.randint(second_key, (block_count, block_count), 0, 4)
    row_ids = jnp.arange(block_count)[:, None]
    col_ids = jnp.arange(block_count)[None, :]
    below = (col_ids < row_ids) & (coins < levels)
    return jnp.where((col_ids == row_ids) | below, 1, 0).astype(jnp.int32)


def level_of(stream_key, shape, cuts, least, high):
    level = 1.0
    for dim, parts in cuts:
        steps = jax.random.uniform(jax.random.fold_in(jax.random.fold_in(stream_key, 6), dim), (parts,), jnp.float32, least / len(cuts), high / len(cuts))
        level = level * jnp.repeat(jnp.exp(steps), shape[dim] // parts).reshape((-1,) + (1,) * (len(shape) - 1 - dim))
    return level


def bell_draw(stream_key, shape, width, reach, cuts=(), held_as=jnp.bfloat16):
    drawn = jax.random.normal(stream_key, shape, jnp.float32) * width
    if len(cuts) > 0:
        drawn = level_of(stream_key, shape, cuts, -0.22, 0.18) * drawn
    return jnp.clip(drawn, min=-reach, max=reach).astype(held_as)


def setup_inputs(seed: int = 0) -> dict:
    key_of = jax.random.split(jax.random.key(seed), 8)
    inputs = bell_draw(key_of[0], (TOKENS, D), 1.0, 6.0, ((0, 32), (1, 16)))
    queries = draw_queries(jax.random.fold_in(key_of[7], 71), 0)
    keys = draw_keys(jax.random.fold_in(key_of[7], 71), 0)
    values = bell_draw(key_of[3], (TOKENS, KVH * HD), 1.0, 6.0, ((0, 16),))
    outputs = bell_draw(key_of[4], (TOKENS, HQ * HD), 0.1, 0.59765625, ((0, 16), (1, 32)))
    out_grad = bell_draw(key_of[5], (TOKENS, HQ * HD), 1.0, 6.0, ((0, 16), (1, 32)))
    block_mask = draw_block_mask(jax.random.fold_in(key_of[7], 71), 0)
    return {"inputs": inputs, "queries": queries, "keys": keys, "values": values, "outputs": outputs, "out_grad": out_grad, "block_mask": block_mask}


def reference(inputs, queries, keys, values, outputs, out_grad, block_mask):
    score_scale = HD ** -0.5
    seq_pos = jnp.arange(TOKENS, dtype=jnp.int32)
    block_ids = seq_pos // BLK
    allowed = (seq_pos[None, :] <= seq_pos[:, None]) & (block_mask[block_ids][:, block_ids] == 1)
    per_group = N_HEAD // KVH
    per_device = HQ // N_HEAD

    def device_work(device):
        kv_group = (device * per_device) // (HQ // KVH)
        key_rows = lax.dynamic_slice_in_dim(keys, (kv_group * HD).astype(jnp.int32), HD, 1)
        value_rows = lax.dynamic_slice_in_dim(values, (kv_group * HD).astype(jnp.int32), HD, 1)
        key_total = jnp.zeros((TOKENS, HD), jnp.float32)
        value_total = jnp.zeros((TOKENS, HD), jnp.float32)
        grads = []
        for head_slot in range(per_device):
            start = ((device * per_device + head_slot) * HD).astype(jnp.int32)
            query_head = lax.dynamic_slice_in_dim(queries, start, HD, 1)
            grad_head = lax.dynamic_slice_in_dim(out_grad, start, HD, 1)
            out_head = lax.dynamic_slice_in_dim(outputs, start, HD, 1)
            scores = jnp.dot(query_head, key_rows.T, preferred_element_type=jnp.float32) * score_scale
            scores = jnp.where(allowed, scores, -jnp.inf)
            row_max = jnp.max(scores, axis=1, keepdims=True)
            row_sum = jnp.sum(jnp.exp(scores - row_max), axis=1, keepdims=True)
            probs = jnp.exp(scores - (row_max + jnp.log(row_sum)))
            probs_low = probs.astype(jnp.bfloat16)
            dprobs = jnp.dot(grad_head, value_rows.T, preferred_element_type=jnp.float32)
            delta = jnp.sum(grad_head.astype(jnp.float32) * out_head.astype(jnp.float32), axis=1, keepdims=True)
            dscores = (probs * (dprobs - delta) * score_scale).astype(jnp.bfloat16)
            grads.append(jnp.dot(dscores, key_rows, preferred_element_type=jnp.float32).astype(jnp.bfloat16))
            key_total = key_total + jnp.dot(dscores.T, query_head, preferred_element_type=jnp.float32)
            value_total = value_total + jnp.dot(probs_low.T, grad_head, preferred_element_type=jnp.float32)
        summed = jnp.concatenate([key_total, value_total], axis=1).astype(jnp.bfloat16)
        return jnp.concatenate(grads, axis=1), summed

    dq_parts, summed_parts = lax.map(device_work, jnp.arange(N_HEAD, dtype=jnp.int32))
    q_grad = jnp.transpose(dq_parts, (1, 0, 2)).reshape(TOKENS, HQ * HD)
    grouped = summed_parts.astype(jnp.float32).reshape(KVH, per_group, TOKENS, 2 * HD)
    kv_heads = jnp.sum(grouped, axis=1).astype(jnp.bfloat16)
    kv_grad = jnp.transpose(kv_heads, (1, 0, 2)).reshape(TOKENS, 2 * KVH * HD)
    weight_q_grad = jnp.dot(inputs.T, q_grad, preferred_element_type=jnp.float32).astype(jnp.bfloat16)
    weight_kv_grad = jnp.dot(inputs.T, kv_grad, preferred_element_type=jnp.float32).astype(jnp.bfloat16)
    return q_grad, kv_grad, weight_q_grad, weight_kv_grad
```

```python
import functools

import jax
import jax.numpy as jnp
from jax import lax
from jax.experimental import pallas as pl
from jax.experimental.pallas import tpu as pltpu
from jax.sharding import PartitionSpec as P

HD = 128
BLK = 64
TOK = 2048
SHARD = 128
CHUNK = 256
MESH = pl.DeviceIdType.MESH
NEG = -1e30
F32 = jnp.float32
BF16 = jnp.bfloat16

PEERS = (
    [(d, 0, 0, 0, 0) for d in (1, 2, 3)]
    + [(0, d, 0, 0, 0) for d in (1, 2, 3)]
    + [(0, 0, d, 0, 0) for d in (1, 2, 3)]
    + [(0, 0, 0, d, 0) for d in (1, 2, 3)]
    + [(0, 0, 0, 0, 1)]
)


def dot(left, right):
    return lax.dot_general(left, right, (((1,), (0,)), ((), ())), preferred_element_type=F32)


def dot_t(left, right):
    return lax.dot_general(left, right, (((1,), (1,)), ((), ())), preferred_element_type=F32)


def stacked(value):
    return jnp.concatenate([value[:, :HD], value[:, HD:]], axis=0)


def body(
    inputs, queries, keys, values, outputs, out_grad, block_mask,
    q_out, kv_out, wq_out, wkv_out,
    act, kv_all, q_all, g_all, scores, probs, dsc, bias,
    sib_send, sib_recv, own, y_send, y_recv, zx_send, zx_recv,
    send_sem, recv_sem, local_sem,
):
    ctx = lax.axis_index("ctx")
    head = lax.axis_index("head")
    z, y = ctx // 4, ctx % 4
    zh, x, core = head // 8, (head // 2) % 4, head % 2
    sib = 1 - core
    side = x % 2
    group = head // 4

    def at(dz=0, dy=0, dzh=0, dx=0, dk=0):
        return (
            ((z + dz) % 4) * 4 + (y + dy) % 4,
            ((zh + dzh) % 4) * 8 + ((x + dx) % 4) * 2 + (core + dk) % 2,
        )

    def flip(dz):
        return (((z + dz) % 4) * 4 + y, zh * 8 + (x + 1 - 2 * side) * 2 + core)

    counter = [0]
    sends = []

    def slots(count):
        first = counter[0]
        counter[0] += count
        return first

    def copy(src, dst, slot, device):
        return pltpu.make_async_remote_copy(
            src_ref=src, dst_ref=dst, send_sem=send_sem.at[slot], recv_sem=recv_sem.at[slot],
            device_id=device, device_id_type=MESH,
        )

    def send(src, dst, slot, device):
        item = copy(src, dst, slot, device)
        item.start()
        sends.append(item)

    def arrive(dst, slot):
        copy(dst, dst, slot, at(dk=1)).wait_recv()

    own_rows = pl.ds(pl.multiple_of(ctx * SHARD, SHARD), SHARD)
    own_cols = pl.ds(pl.multiple_of(group * HD, HD), HD)
    own_act = pl.ds(pl.multiple_of(head * 64, 64), 64)
    loads = [
        pltpu.make_async_copy(keys.at[:, own_cols], kv_all.at[0, own_rows], local_sem.at[0]),
        pltpu.make_async_copy(values.at[:, own_cols], kv_all.at[1, own_rows], local_sem.at[1]),
        pltpu.make_async_copy(inputs, act.at[own_act], local_sem.at[2]),
    ]
    for item in loads:
        item.start()

    barrier = pltpu.get_barrier_semaphore()
    for offset in PEERS:
        pl.semaphore_signal(barrier, inc=1, device_id=at(*offset), device_id_type=MESH)
    for dz in (1, 2, 3):
        pl.semaphore_signal(barrier, inc=1, device_id=flip(dz), device_id_type=MESH)
    for item in loads:
        item.wait()
    pl.semaphore_wait(barrier, len(PEERS) + 3)

    class Gather:
        def __init__(self, place):
            self.place = place
            self.first = slots(16)

        def shard(self, dz, dy):
            return self.place(((z - dz) % 4) * 4 + (y - dy) % 4)

        def start(self):
            for dz in (1, 3, 2):
                send(self.shard(0, 0), self.shard(0, 0), self.first + dz * 4, at(dz=dz))
            self.along_y(0)

        def along_y(self, dz):
            for dy in (1, 3, 2):
                send(self.shard(dz, 0), self.shard(dz, 0), self.first + dz * 4 + dy, at(dy=dy))

        def wait(self, dz, dy):
            arrive(self.shard(dz, dy), self.first + dz * 4 + dy)

    def rows_of(index):
        return pl.ds(pl.multiple_of(index * SHARD, SHARD), SHARD)

    kv_gather = Gather(lambda index: kv_all.at[core, rows_of(index)])
    kv_gather.start()
    sib_first = slots(16)

    def to_sibling(dz, dy):
        part = kv_gather.shard(dz, dy)
        send(part, part, sib_first + dz * 4 + dy, at(dk=1))

    row_ids = lax.broadcasted_iota(jnp.int32, (2 * SHARD, CHUNK), 0) % SHARD + ctx * SHARD
    pick = (
        lax.broadcasted_iota(jnp.int32, (2 * SHARD, 32), 1)
        == (lax.broadcasted_iota(jnp.int32, (2 * SHARD, 32), 0) % SHARD + ctx * SHARD) // BLK
    )
    mask_rows = dot(pick.astype(BF16), block_mask[...].astype(BF16)).astype(BF16)

    def bias_step(step, carry):
        cols = pl.ds(pl.multiple_of(step * CHUNK, CHUNK), CHUNK)
        col_ids = lax.broadcasted_iota(jnp.int32, (2 * SHARD, CHUNK), 1) + step * CHUNK
        spread = (
            (lax.broadcasted_iota(jnp.int32, (32, CHUNK), 1) + step * CHUNK) // BLK
            == lax.broadcasted_iota(jnp.int32, (32, CHUNK), 0)
        )
        wide = dot(mask_rows, spread.astype(BF16))
        bias[:, cols] = jnp.where((wide > 0.5) & (col_ids <= row_ids), 0.0, NEG)
        return carry

    lax.fori_loop(0, TOK // CHUNK, bias_step, 0)
    query = stacked(queries[...])
    grad = stacked(out_grad[...])
    delta = jnp.sum(grad.astype(F32) * stacked(outputs[...]).astype(F32), axis=1, keepdims=True)

    for dz in (1, 3, 2):
        kv_gather.wait(dz, 0)
        kv_gather.along_y(dz)
        to_sibling(dz, 0)

    act_first = slots(16)
    act_sib = slots(16)

    def act_shard(dzh, dx):
        index = ((zh - dzh) % 4) * 8 + ((x - dx) % 4) * 2 + core
        return act.at[pl.ds(pl.multiple_of(index * 64, 64), 64)]

    def act_from_sibling(dzh, dx):
        index = ((zh - dzh) % 4) * 8 + ((x - dx) % 4) * 2 + sib
        return act.at[pl.ds(pl.multiple_of(index * 64, 64), 64)]

    def act_along_x(dzh):
        for dx in (1, 3, 2):
            send(act_shard(dzh, 0), act_shard(dzh, 0), act_first + dzh * 4 + dx, at(dx=dx))
        act_to_sibling(dzh, 0)

    def act_to_sibling(dzh, dx):
        send(act_shard(dzh, dx), act_shard(dzh, dx), act_sib + dzh * 4 + dx, at(dk=1))

    for dzh in (1, 3, 2):
        send(act_shard(0, 0), act_shard(0, 0), act_first + dzh * 4, at(dzh=dzh))
    act_along_x(0)

    for dz in range(4):
        for dy in (1, 3, 2):
            kv_gather.wait(dz, dy)
            to_sibling(dz, dy)
    for dz in range(4):
        for dy in range(4):
            if dz or dy:
                index = ((z - dz) % 4) * 4 + (y - dy) % 4
                arrive(kv_all.at[sib, rows_of(index)], sib_first + dz * 4 + dy)

    scale = HD ** -0.5

    def score_step(step, top):
        cols = pl.ds(pl.multiple_of(step * CHUNK, CHUNK), CHUNK)
        part = dot_t(query, kv_all[0, cols, :]) * scale + bias[:, cols]
        scores[:, cols] = part
        return jnp.maximum(top, jnp.maximum(part[:, :HD], part[:, HD:]))

    top = lax.fori_loop(0, TOK // CHUNK, score_step, jnp.full((2 * SHARD, HD), NEG, F32))
    row_max = jnp.max(top, axis=1, keepdims=True)

    def prob_step(step, total):
        cols = pl.ds(pl.multiple_of(step * CHUNK, CHUNK), CHUNK)
        part = jnp.exp(scores[:, cols] - row_max)
        slope = dot_t(grad, kv_all[1, cols, :])
        probs[:, cols] = part.astype(BF16)
        dsc[:, cols] = (part * (slope - delta)).astype(BF16)
        return total + part[:, :HD] + part[:, HD:]

    total = lax.fori_loop(0, TOK // CHUNK, prob_step, jnp.zeros((2 * SHARD, HD), F32))
    inverse = 1.0 / jnp.sum(total, axis=1, keepdims=True)

    def mine_first(value):
        turned = value.T
        low, high = turned[:64], turned[64:]
        return jnp.concatenate(
            [jnp.where(core == 0, low, high), jnp.where(core == 0, high, low)], axis=0
        ).astype(BF16)

    query_t = mine_first(query.astype(F32) * (inverse * scale))
    grad_t = mine_first(grad.astype(F32) * inverse)

    def term_step(step, carry):
        cols = pl.ds(pl.multiple_of(step * CHUNK, CHUNK), CHUNK)
        key_part = dot(query_t, dsc[:, cols])
        value_part = dot(grad_t, probs[:, cols])
        for half in range(2):
            index = step * 2 + half
            block = (index % 4) * 4 + index // 4
            lanes = slice(half * HD, (half + 1) * HD)
            own[block, 0] = key_part[:64, lanes]
            own[block, 1] = value_part[:64, lanes]
            sib_send[block, 0] = key_part[64:, lanes].astype(BF16)
            sib_send[block, 1] = value_part[64:, lanes].astype(BF16)
        return carry

    lax.fori_loop(0, TOK // CHUNK, term_step, 0)
    core_slot = slots(1)
    send(sib_send, sib_recv, core_slot, at(dk=1))

    query_grad = dot(dsc[...], kv_all[0]) * (inverse * scale)
    q_out[:, :HD] = query_grad[:SHARD].astype(BF16)
    q_out[:, HD:] = query_grad[SHARD:].astype(BF16)
    own_lanes = pl.ds(pl.multiple_of(ctx * SHARD, SHARD), SHARD)
    q_all[:HD, own_lanes] = query_grad[:SHARD].T.astype(BF16)
    q_all[HD:, own_lanes] = query_grad[SHARD:].T.astype(BF16)

    arrive(sib_recv, core_slot)
    y_slot = slots(4)
    for dy in (1, 3, 2):
        dest = (y + dy) % 4

        def add_step(step, carry):
            block = dest * 4 + step
            y_send[dy - 1, step] = (own[block] + sib_recv[block].astype(F32)).astype(BF16)
            return carry

        lax.fori_loop(0, 4, add_step, 0)
        send(y_send.at[dy - 1], y_recv.at[dy - 1], y_slot + dy, at(dy=dy))

    def lanes_of(index):
        return pl.ds(pl.multiple_of(index * SHARD, SHARD), SHARD)

    q_gather = Gather(lambda index: q_all.at[:, lanes_of(index)])
    q_gather.start()

    for dzh in (1, 3, 2):
        arrive(act_shard(dzh, 0), act_first + dzh * 4)
        act_along_x(dzh)

    for dy in (1, 3, 2):
        arrive(y_recv.at[dy - 1], y_slot + dy)

    def y_sum(step, carry):
        block = y * 4 + step
        value = own[block] + sib_recv[block].astype(F32)
        for dy in (1, 2, 3):
            value = value + y_recv[dy - 1, step].astype(F32)
        own[block] = value
        zx_send[step] = value.astype(BF16)
        return carry

    lax.fori_loop(0, 4, y_sum, 0)

    zx_slot = slots(8)
    for dz in (1, 3, 2, 0):
        for dx in (0, 1):
            if dz or dx:
                part = side if dx == 0 else 1 - side
                slot = dz * 2 + dx
                send(
                    zx_send.at[(z + dz) % 4, part], zx_recv.at[slot], zx_slot + slot,
                    flip(dz) if dx else at(dz=dz),
                )

    for dz in (1, 3, 2):
        q_gather.wait(dz, 0)
        q_gather.along_y(dz)

    kv_sum = own[y * 4 + z, side]
    for slot in range(1, 8):
        arrive(zx_recv.at[slot], zx_slot + slot)
    for slot in range(1, 8):
        kv_sum = kv_sum + zx_recv[slot].astype(F32)
    g_all[:, own_lanes] = kv_sum.astype(BF16)
    g_gather = Gather(lambda index: g_all.at[:, lanes_of(index)])
    g_gather.start()
    kv_out[...] = kv_sum.T.astype(BF16)

    for dzh in range(4):
        for dx in (1, 3, 2):
            arrive(act_shard(dzh, dx), act_first + dzh * 4 + dx)
            act_to_sibling(dzh, dx)

    for dz in (1, 3, 2):
        g_gather.wait(dz, 0)
        g_gather.along_y(dz)

    for dz in range(4):
        for dy in (1, 3, 2):
            q_gather.wait(dz, dy)
    for dzh in range(4):
        for dx in range(4):
            arrive(act_from_sibling(dzh, dx), act_sib + dzh * 4 + dx)
    wq_out[...] = dot(q_all[...], act[...]).T.astype(BF16)

    for dz in range(4):
        for dy in (1, 3, 2):
            g_gather.wait(dz, dy)
    wkv_out[...] = dot(g_all[...], act[...]).T.astype(BF16)

    for item in sends:
        item.wait_send()


def per_device(inputs, queries, keys, values, outputs, out_grad, block_mask):
    vmem = pl.BlockSpec(memory_space=pltpu.VMEM)
    anywhere = pl.BlockSpec(memory_space=pl.ANY)
    return pl.pallas_call(
        body,
        name="attention_backward",
        out_shape=(
            jax.ShapeDtypeStruct((SHARD, 256), BF16),
            jax.ShapeDtypeStruct((SHARD, 64), BF16),
            jax.ShapeDtypeStruct((512, 256), BF16),
            jax.ShapeDtypeStruct((512, 64), BF16),
        ),
        in_specs=[anywhere, vmem, anywhere, anywhere, vmem, vmem, vmem],
        out_specs=(vmem, vmem, vmem, vmem),
        scratch_shapes=[
            pltpu.VMEM((TOK, 512), BF16),
            pltpu.VMEM((2, TOK, HD), BF16),
            pltpu.VMEM((256, TOK), BF16),
            pltpu.VMEM((64, TOK), BF16),
            pltpu.VMEM((256, TOK), F32),
            pltpu.VMEM((256, TOK), BF16),
            pltpu.VMEM((256, TOK), BF16),
            pltpu.VMEM((256, TOK), F32),
            pltpu.VMEM((16, 2, 64, HD), BF16),
            pltpu.VMEM((16, 2, 64, HD), BF16),
            pltpu.VMEM((16, 2, 64, HD), F32),
            pltpu.VMEM((3, 4, 2, 64, HD), BF16),
            pltpu.VMEM((3, 4, 2, 64, HD), BF16),
            pltpu.VMEM((4, 2, 64, HD), BF16),
            pltpu.VMEM((8, 64, HD), BF16),
            pltpu.SemaphoreType.DMA((112,)),
            pltpu.SemaphoreType.DMA((112,)),
            pltpu.SemaphoreType.DMA((3,)),
        ],
        compiler_params=pltpu.CompilerParams(
            collective_id=0, has_side_effects=True, vmem_limit_bytes=48 << 20
        ),
        cost_estimate=pl.CostEstimate(
            flops=1_400_000_000, bytes_accessed=4 << 20, transcendentals=256 * TOK
        ),
    )(inputs, queries, keys, values, outputs, out_grad, block_mask)


def solution(mesh):
    in_specs = (
        P("head", "ctx"),
        P("ctx", "head"),
        P("ctx", None),
        P("ctx", None),
        P("ctx", "head"),
        P("ctx", "head"),
        P(),
    )
    out_specs = (P("ctx", "head"), P("ctx", "head"), P("ctx", "head"), P("ctx", "head"))
    return jax.shard_map(
        per_device, mesh=mesh, in_specs=in_specs, out_specs=out_specs, check_vma=False
    )
```

```python
import functools

import jax
import jax.numpy as jnp
from jax import lax
from jax.experimental import pallas as pl
from jax.experimental.pallas import tpu as pltpu
from jax.sharding import PartitionSpec as P

HD = 128
BLK = 64
TOK = 2048
SHARD = 128
CHUNK = 256
MESH = pl.DeviceIdType.MESH
NEG = -1e30
VMEM_LIMIT = 60 << 20
F32 = jnp.float32
BF16 = jnp.bfloat16

PEERS = (
    [(d, 0, 0, 0, 0) for d in (1, 2, 3)]
    + [(0, d, 0, 0, 0) for d in (1, 2, 3)]
    + [(0, 0, 0, d, 0) for d in (1, 2, 3)]
    + [(0, 0, 0, 0, 1)]
)


def dot(left, right):
    return lax.dot_general(left, right, (((1,), (0,)), ((), ())), preferred_element_type=F32)


def dot_t(left, right):
    return lax.dot_general(left, right, (((1,), (1,)), ((), ())), preferred_element_type=F32)


def stacked(value):
    return jnp.concatenate([value[:, :HD], value[:, HD:]], axis=0)


def body(
    inputs, queries, keys, values, outputs, out_grad, block_mask,
    q_out, kv_out, wq_out, wkv_out,
    query_in, grad_in, out_in, mask_in,
    act, kv_all, q_all, g_all, scores, probs, dsc, bias,
    sib_send, sib_recv, own, y_send, y_recv, zx_send, zx_recv,
    send_sem, recv_sem, local_sem, ready_sem,
):
    ctx = lax.axis_index("ctx")
    head = lax.axis_index("head")
    z, y = ctx // 4, ctx % 4
    zh, x, core = head // 8, (head // 2) % 4, head % 2
    sib = 1 - core
    side = x % 2
    group = head // 4

    def at(dz=0, dy=0, dzh=0, dx=0, dk=0):
        return (
            ((z + dz) % 4) * 4 + (y + dy) % 4,
            ((zh + dzh) % 4) * 8 + ((x + dx) % 4) * 2 + (core + dk) % 2,
        )

    def flip(dz):
        return (((z + dz) % 4) * 4 + y, zh * 8 + (x + 1 - 2 * side) * 2 + core)

    counter = [0]
    sends = []

    def slots(count):
        first = counter[0]
        counter[0] += count
        return first

    def copy(src, dst, slot, device):
        return pltpu.make_async_remote_copy(
            src_ref=src, dst_ref=dst, send_sem=send_sem.at[slot], recv_sem=recv_sem.at[slot],
            device_id=device, device_id_type=MESH,
        )

    def send(src, dst, slot, device):
        item = copy(src, dst, slot, device)
        item.start()
        sends.append(item)

    def arrive(dst, slot):
        copy(dst, dst, slot, at(dk=1)).wait_recv()

    own_rows = pl.ds(pl.multiple_of(ctx * SHARD, SHARD), SHARD)
    own_cols = pl.ds(pl.multiple_of(group * HD, HD), HD)
    own_act = pl.ds(pl.multiple_of(head * 64, 64), 64)
    loads = [
        pltpu.make_async_copy(keys.at[:, own_cols], kv_all.at[0, own_rows], local_sem.at[0]),
        pltpu.make_async_copy(values.at[:, own_cols], kv_all.at[1, own_rows], local_sem.at[1]),
        pltpu.make_async_copy(inputs, act.at[own_act], local_sem.at[2]),
        pltpu.make_async_copy(block_mask, mask_in, local_sem.at[3]),
        pltpu.make_async_copy(queries, query_in, local_sem.at[4]),
        pltpu.make_async_copy(out_grad, grad_in, local_sem.at[5]),
        pltpu.make_async_copy(outputs, out_in, local_sem.at[6]),
    ]
    for item in loads:
        item.start()

    barrier = pltpu.get_barrier_semaphore()
    for offset in PEERS:
        pl.semaphore_signal(barrier, inc=1, device_id=at(*offset), device_id_type=MESH)
    for dz in (1, 2, 3):
        pl.semaphore_signal(barrier, inc=1, device_id=flip(dz), device_id_type=MESH)
    def rank_of(index):
        return jnp.where(index < 2, index, 5 - index)

    rank = rank_of(zh)
    ranks = {dzh: rank_of((zh + dzh) % 4) for dzh in (1, 2, 3)}
    for dzh in (1, 2, 3):
        @pl.when(rank < ranks[dzh])
        def _(dzh=dzh):
            pl.semaphore_signal(barrier, inc=1, device_id=at(dzh=dzh), device_id_type=MESH)

    for item in loads[:3]:
        item.wait()
    pl.semaphore_wait(barrier, len(PEERS) + 3 + rank)

    class Gather:
        def __init__(self, place):
            self.place = place
            self.first = slots(16)

        def shard(self, dz, dy):
            return self.place(((z - dz) % 4) * 4 + (y - dy) % 4)

        def start(self):
            for dz in (1, 3, 2):
                send(self.shard(0, 0), self.shard(0, 0), self.first + dz * 4, at(dz=dz))
            self.along_y(0)

        def along_y(self, dz):
            for dy in (1, 3, 2):
                send(self.shard(dz, 0), self.shard(dz, 0), self.first + dz * 4 + dy, at(dy=dy))

        def wait(self, dz, dy):
            arrive(self.shard(dz, dy), self.first + dz * 4 + dy)

    def rows_of(index):
        return pl.ds(pl.multiple_of(index * SHARD, SHARD), SHARD)

    kv_gather = Gather(lambda index: kv_all.at[core, rows_of(index)])
    kv_gather.start()
    sib_first = slots(16)

    def to_sibling(dz, dy):
        part = kv_gather.shard(dz, dy)
        send(part, part, sib_first + dz * 4 + dy, at(dk=1))

    act_first = slots(16)
    act_sib = slots(16)

    def act_shard(dzh, dx):
        index = ((zh - dzh) % 4) * 8 + ((x - dx) % 4) * 2 + core
        return act.at[pl.ds(pl.multiple_of(index * 64, 64), 64)]

    def act_from_sibling(dzh, dx):
        index = ((zh - dzh) % 4) * 8 + ((x - dx) % 4) * 2 + sib
        return act.at[pl.ds(pl.multiple_of(index * 64, 64), 64)]

    def act_along_x(dzh):
        for dx in (1, 3, 2):
            send(act_shard(dzh, 0), act_shard(dzh, 0), act_first + dzh * 4 + dx, at(dx=dx))
        act_to_sibling(dzh, 0)

    def act_to_sibling(dzh, dx):
        send(act_shard(dzh, dx), act_shard(dzh, dx), act_sib + dzh * 4 + dx, at(dk=1))

    def act_along_z(dzh):
        return copy(act_shard(0, 0), act_shard(0, 0), act_first + dzh * 4, at(dzh=dzh))

    for dzh in (1, 3, 2):
        sends.append(act_along_z(dzh))

        @pl.when(rank > ranks[dzh])
        def _(dzh=dzh):
            pl.semaphore_signal(ready_sem.at[dzh], inc=1, device_id=at(dzh=dzh), device_id_type=MESH)
            act_along_z(dzh).start()

    for item in loads[3:]:
        item.wait()
    row_ids = lax.broadcasted_iota(jnp.int32, (2 * SHARD, CHUNK), 0) % SHARD + ctx * SHARD
    pick = (
        lax.broadcasted_iota(jnp.int32, (2 * SHARD, 32), 1)
        == (lax.broadcasted_iota(jnp.int32, (2 * SHARD, 32), 0) % SHARD + ctx * SHARD) // BLK
    )
    mask_rows = dot(pick.astype(BF16), mask_in[...].astype(BF16)).astype(BF16)

    def bias_step(step, carry):
        cols = pl.ds(pl.multiple_of(step * CHUNK, CHUNK), CHUNK)
        col_ids = lax.broadcasted_iota(jnp.int32, (2 * SHARD, CHUNK), 1) + step * CHUNK
        spread = (
            (lax.broadcasted_iota(jnp.int32, (32, CHUNK), 1) + step * CHUNK) // BLK
            == lax.broadcasted_iota(jnp.int32, (32, CHUNK), 0)
        )
        wide = dot(mask_rows, spread.astype(BF16))
        bias[:, cols] = jnp.where((wide > 0.5) & (col_ids <= row_ids), 0.0, NEG)
        return carry

    lax.fori_loop(0, TOK // CHUNK, bias_step, 0)
    query = stacked(query_in[...])
    grad = stacked(grad_in[...])
    delta = jnp.sum(grad.astype(F32) * stacked(out_in[...]).astype(F32), axis=1, keepdims=True)

    for dz in (1, 3, 2):
        kv_gather.wait(dz, 0)
        kv_gather.along_y(dz)
        to_sibling(dz, 0)

    act_along_x(0)

    for dz in range(4):
        for dy in (1, 3, 2):
            kv_gather.wait(dz, dy)
            to_sibling(dz, dy)
    for dz in range(4):
        for dy in range(4):
            if dz or dy:
                index = ((z - dz) % 4) * 4 + (y - dy) % 4
                arrive(kv_all.at[sib, rows_of(index)], sib_first + dz * 4 + dy)

    scale = HD ** -0.5

    def score_step(step, top):
        cols = pl.ds(pl.multiple_of(step * CHUNK, CHUNK), CHUNK)
        part = dot_t(query, kv_all[0, cols, :]) * scale + bias[:, cols]
        scores[:, cols] = part
        return jnp.maximum(top, jnp.maximum(part[:, :HD], part[:, HD:]))

    top = lax.fori_loop(0, TOK // CHUNK, score_step, jnp.full((2 * SHARD, HD), NEG, F32))
    row_max = jnp.max(top, axis=1, keepdims=True)

    def prob_step(step, total):
        cols = pl.ds(pl.multiple_of(step * CHUNK, CHUNK), CHUNK)
        part = jnp.exp(scores[:, cols] - row_max)
        slope = dot_t(grad, kv_all[1, cols, :])
        probs[:, cols] = part.astype(BF16)
        dsc[:, cols] = (part * (slope - delta)).astype(BF16)
        return total + part[:, :HD] + part[:, HD:]

    total = lax.fori_loop(0, TOK // CHUNK, prob_step, jnp.zeros((2 * SHARD, HD), F32))
    inverse = 1.0 / jnp.sum(total, axis=1, keepdims=True)

    def mine_first(value):
        turned = value.T
        low, high = turned[:64], turned[64:]
        return jnp.concatenate(
            [jnp.where(core == 0, low, high), jnp.where(core == 0, high, low)], axis=0
        ).astype(BF16)

    query_t = mine_first(query.astype(F32) * (inverse * scale))
    grad_t = mine_first(grad.astype(F32) * inverse)

    def term_step(step, carry):
        cols = pl.ds(pl.multiple_of(step * CHUNK, CHUNK), CHUNK)
        key_part = dot(query_t, dsc[:, cols])
        value_part = dot(grad_t, probs[:, cols])
        for half in range(2):
            index = step * 2 + half
            block = (index % 4) * 4 + index // 4
            lanes = slice(half * HD, (half + 1) * HD)
            own[block, 0] = key_part[:64, lanes]
            own[block, 1] = value_part[:64, lanes]
            sib_send[block, 0] = key_part[64:, lanes].astype(BF16)
            sib_send[block, 1] = value_part[64:, lanes].astype(BF16)
        return carry

    lax.fori_loop(0, TOK // CHUNK, term_step, 0)
    core_slot = slots(1)
    send(sib_send, sib_recv, core_slot, at(dk=1))

    query_grad = dot(dsc[...], kv_all[0]) * (inverse * scale)
    q_out[:, :HD] = query_grad[:SHARD].astype(BF16)
    q_out[:, HD:] = query_grad[SHARD:].astype(BF16)
    own_lanes = pl.ds(pl.multiple_of(ctx * SHARD, SHARD), SHARD)
    q_all[:HD, own_lanes] = query_grad[:SHARD].T.astype(BF16)
    q_all[HD:, own_lanes] = query_grad[SHARD:].T.astype(BF16)

    for dzh in (1, 3, 2):
        @pl.when(rank < ranks[dzh])
        def _(dzh=dzh):
            pl.semaphore_wait(ready_sem.at[4 - dzh], 1)
            act_along_z(dzh).start()

    arrive(sib_recv, core_slot)
    y_slot = slots(4)
    for dy in (1, 3, 2):
        dest = (y + dy) % 4

        def add_step(step, carry):
            block = dest * 4 + step
            y_send[dy - 1, step] = (own[block] + sib_recv[block].astype(F32)).astype(BF16)
            return carry

        lax.fori_loop(0, 4, add_step, 0)
        send(y_send.at[dy - 1], y_recv.at[dy - 1], y_slot + dy, at(dy=dy))

    def lanes_of(index):
        return pl.ds(pl.multiple_of(index * SHARD, SHARD), SHARD)

    q_gather = Gather(lambda index: q_all.at[:, lanes_of(index)])
    q_gather.start()

    for dzh in (1, 3, 2):
        arrive(act_shard(dzh, 0), act_first + dzh * 4)
        act_along_x(dzh)

    for dy in (1, 3, 2):
        arrive(y_recv.at[dy - 1], y_slot + dy)

    def y_sum(step, carry):
        block = y * 4 + step
        value = own[block] + sib_recv[block].astype(F32)
        for dy in (1, 2, 3):
            value = value + y_recv[dy - 1, step].astype(F32)
        own[block] = value
        zx_send[step] = value.astype(BF16)
        return carry

    lax.fori_loop(0, 4, y_sum, 0)

    zx_slot = slots(8)
    for dz in (1, 3, 2, 0):
        for dx in (0, 1):
            if dz or dx:
                part = side if dx == 0 else 1 - side
                slot = dz * 2 + dx
                send(
                    zx_send.at[(z + dz) % 4, part], zx_recv.at[slot], zx_slot + slot,
                    flip(dz) if dx else at(dz=dz),
                )

    for dz in (1, 3, 2):
        q_gather.wait(dz, 0)
        q_gather.along_y(dz)

    kv_sum = own[y * 4 + z, side]
    for slot in range(1, 8):
        arrive(zx_recv.at[slot], zx_slot + slot)
    for slot in range(1, 8):
        kv_sum = kv_sum + zx_recv[slot].astype(F32)
    g_all[:, own_lanes] = kv_sum.astype(BF16)
    g_gather = Gather(lambda index: g_all.at[:, lanes_of(index)])
    g_gather.start()
    kv_out[...] = kv_sum.astype(BF16)

    for dzh in range(4):
        for dx in (1, 3, 2):
            arrive(act_shard(dzh, dx), act_first + dzh * 4 + dx)
            act_to_sibling(dzh, dx)

    for dz in (1, 3, 2):
        g_gather.wait(dz, 0)
        g_gather.along_y(dz)

    for dz in range(4):
        for dy in (1, 3, 2):
            q_gather.wait(dz, dy)
    for dzh in range(4):
        for dx in range(4):
            arrive(act_from_sibling(dzh, dx), act_sib + dzh * 4 + dx)
    wq_out[...] = dot(q_all[...], act[...]).T.astype(BF16)

    for dz in range(4):
        for dy in (1, 3, 2):
            g_gather.wait(dz, dy)
    wkv_out[...] = dot(g_all[...], act[...]).astype(BF16)

    for item in sends:
        item.wait_send()


def deliver(*refs):
    for source, result in zip(refs[:4], refs[4:]):
        result[...] = source[...]


def per_device(inputs, queries, keys, values, outputs, out_grad, block_mask):
    vmem = pl.BlockSpec(memory_space=pltpu.VMEM)
    anywhere = pl.BlockSpec(memory_space=pl.ANY)
    shapes = (
        jax.ShapeDtypeStruct((SHARD, 256), BF16),
        jax.ShapeDtypeStruct((64, SHARD), BF16),
        jax.ShapeDtypeStruct((512, 256), BF16),
        jax.ShapeDtypeStruct((64, 512), BF16),
    )
    results = pl.pallas_call(
        body,
        name="attention_backward",
        out_shape=shapes,
        in_specs=[anywhere] * 7,
        out_specs=(vmem, vmem, vmem, vmem),
        scratch_shapes=[
            pltpu.VMEM((SHARD, 256), BF16),
            pltpu.VMEM((SHARD, 256), BF16),
            pltpu.VMEM((SHARD, 256), BF16),
            pltpu.VMEM((32, 32), jnp.int32),
            pltpu.VMEM((TOK, 512), BF16),
            pltpu.VMEM((2, TOK, HD), BF16),
            pltpu.VMEM((256, TOK), BF16),
            pltpu.VMEM((64, TOK), BF16),
            pltpu.VMEM((256, TOK), F32),
            pltpu.VMEM((256, TOK), BF16),
            pltpu.VMEM((256, TOK), BF16),
            pltpu.VMEM((256, TOK), F32),
            pltpu.VMEM((16, 2, 64, HD), BF16),
            pltpu.VMEM((16, 2, 64, HD), BF16),
            pltpu.VMEM((16, 2, 64, HD), F32),
            pltpu.VMEM((3, 4, 2, 64, HD), BF16),
            pltpu.VMEM((3, 4, 2, 64, HD), BF16),
            pltpu.VMEM((4, 2, 64, HD), BF16),
            pltpu.VMEM((8, 64, HD), BF16),
            pltpu.SemaphoreType.DMA((112,)),
            pltpu.SemaphoreType.DMA((112,)),
            pltpu.SemaphoreType.DMA((7,)),
            pltpu.SemaphoreType.REGULAR((4,)),
        ],
        compiler_params=pltpu.CompilerParams(
            collective_id=0, has_side_effects=True, vmem_limit_bytes=VMEM_LIMIT
        ),
        cost_estimate=pl.CostEstimate(
            flops=1_400_000_000, bytes_accessed=4 << 20, transcendentals=256 * TOK
        ),
    )(inputs, queries, keys, values, outputs, out_grad, block_mask)
    q_grad, kv_turned, weight_q, weight_kv_turned = pl.pallas_call(
        deliver,
        name="deliver",
        out_shape=shapes,
        in_specs=[vmem] * 4,
        out_specs=[vmem] * 4,
        compiler_params=pltpu.CompilerParams(vmem_limit_bytes=VMEM_LIMIT),
    )(*results)
    return q_grad, kv_turned.T, weight_q, weight_kv_turned.T


def solution(mesh):
    in_specs = (
        P("head", "ctx"),
        P("ctx", "head"),
        P("ctx", None),
        P("ctx", None),
        P("ctx", "head"),
        P("ctx", "head"),
        P(),
    )
    out_specs = (P("ctx", "head"), P("ctx", "head"), P("ctx", "head"), P("ctx", "head"))
    return jax.shard_map(
        per_device, mesh=mesh, in_specs=in_specs, out_specs=out_specs, check_vma=False
    )
```

```python
import functools

import jax
import jax.numpy as jnp
from jax import lax
from jax.experimental import pallas as pl
from jax.experimental.pallas import tpu as pltpu
from jax.sharding import PartitionSpec as P

HD = 128
BLK = 64
TOK = 2048
SHARD = 128
CHUNK = 256
MESH = pl.DeviceIdType.MESH
NEG = -1e30
VMEM_LIMIT = 60 << 20
F32 = jnp.float32
BF16 = jnp.bfloat16

def dot(left, right):
    return lax.dot_general(left, right, (((1,), (0,)), ((), ())), preferred_element_type=F32)


def dot_t(left, right):
    return lax.dot_general(left, right, (((1,), (1,)), ((), ())), preferred_element_type=F32)


def stacked(value):
    return jnp.concatenate([value[:, :HD], value[:, HD:]], axis=0)


def body(
    inputs, queries, keys, values, outputs, out_grad, block_mask,
    q_out, kv_out, wq_out, wkv_out,
    query_in, grad_in, out_in, mask_in,
    act, kv_all, q_all, g_all, scores, slopes, probs, dsc, bias, top,
    sib_send, sib_recv, own, y_send, y_recv, zx_send, zx_recv,
    send_sem, recv_sem, local_sem, ready_sem,
):
    ctx = lax.axis_index("ctx")
    head = lax.axis_index("head")
    z, y = ctx // 4, ctx % 4
    zh, x, core = head // 8, (head // 2) % 4, head % 2
    sib = 1 - core
    side = x % 2
    group = head // 4

    def at(dz=0, dy=0, dzh=0, dx=0, dk=0):
        return (
            ((z + dz) % 4) * 4 + (y + dy) % 4,
            ((zh + dzh) % 4) * 8 + ((x + dx) % 4) * 2 + (core + dk) % 2,
        )

    def flip(dz):
        return (((z + dz) % 4) * 4 + y, zh * 8 + (x + 1 - 2 * side) * 2 + core)

    counter = [0]
    sends = []

    def slots(count):
        first = counter[0]
        counter[0] += count
        return first

    def copy(src, dst, slot, device):
        return pltpu.make_async_remote_copy(
            src_ref=src, dst_ref=dst, send_sem=send_sem.at[slot], recv_sem=recv_sem.at[slot],
            device_id=device, device_id_type=MESH,
        )

    def send(src, dst, slot, device):
        item = copy(src, dst, slot, device)
        item.start()
        sends.append(item)

    def arrive(dst, slot):
        copy(dst, dst, slot, at(dk=1)).wait_recv()

    def signal(sem, device):
        pl.semaphore_signal(sem, inc=1, device_id=device, device_id_type=MESH)

    own_rows = pl.ds(pl.multiple_of(ctx * SHARD, SHARD), SHARD)
    own_cols = pl.ds(pl.multiple_of(group * HD, HD), HD)
    own_act = pl.ds(pl.multiple_of(head * 64, 64), 64)
    loads = [
        pltpu.make_async_copy(keys.at[:, own_cols], kv_all.at[0, own_rows], local_sem.at[0]),
        pltpu.make_async_copy(values.at[:, own_cols], kv_all.at[1, own_rows], local_sem.at[1]),
        pltpu.make_async_copy(inputs, act.at[own_act], local_sem.at[2]),
        pltpu.make_async_copy(block_mask, mask_in, local_sem.at[3]),
        pltpu.make_async_copy(queries, query_in, local_sem.at[4]),
        pltpu.make_async_copy(out_grad, grad_in, local_sem.at[5]),
        pltpu.make_async_copy(outputs, out_in, local_sem.at[6]),
    ]
    for item in loads:
        item.start()

    def rank_of(index):
        return jnp.where(index < 2, index, 5 - index)

    barrier = pltpu.get_barrier_semaphore()
    for offset in (1, 2, 3):
        signal(barrier, at(dy=offset))
        signal(barrier, at(dz=offset))
    signal(barrier, at(dk=1))

    rank_z, rank_x = rank_of(zh), rank_of(x)
    pair_first = (x == 0) | (x == 3)
    links = {}
    for offset in (1, 2, 3):
        links["z", offset] = (
            rank_z < rank_of((zh + offset) % 4), at(dzh=offset), offset, 4 - offset
        )
        links["x", offset] = (
            rank_x < rank_of((x + offset) % 4), at(dx=offset), 4 + offset, 8 - offset
        )
        links["f", offset] = (pair_first, flip(offset), 8 + offset, 12 - offset)

    for first, device, _, _ in links.values():
        @pl.when(first)
        def _(device=device):
            signal(barrier, device)

    for item in loads[:3]:
        item.wait()
    pl.semaphore_wait(barrier, 7 + rank_z + rank_x + jnp.where(pair_first, 0, 3))

    def answer(key):
        first, device, slot, _ = links[key]

        @pl.when(jnp.logical_not(first))
        def _():
            signal(ready_sem.at[slot], device)

    def await_answer(key):
        first, _, _, slot = links[key]

        @pl.when(first)
        def _():
            pl.semaphore_wait(ready_sem.at[slot], 1)

    class Gather:
        def __init__(self, place):
            self.place = place
            self.first = slots(16)

        def shard(self, dz, dy):
            return self.place(((z - dz) % 4) * 4 + (y - dy) % 4)

        def start(self):
            for dz in (1, 3, 2):
                send(self.shard(0, 0), self.shard(0, 0), self.first + dz * 4, at(dz=dz))
            self.along_y(0)

        def along_y(self, dz):
            for dy in (1, 3, 2):
                send(self.shard(dz, 0), self.shard(dz, 0), self.first + dz * 4 + dy, at(dy=dy))

        def wait(self, dz, dy):
            arrive(self.shard(dz, dy), self.first + dz * 4 + dy)

    def rows_of(index):
        return pl.ds(pl.multiple_of(index * SHARD, SHARD), SHARD)

    kv_gather = Gather(lambda index: kv_all.at[core, rows_of(index)])
    kv_gather.start()
    sib_first = slots(16)

    def to_sibling(dz, dy):
        part = kv_gather.shard(dz, dy)
        send(part, part, sib_first + dz * 4 + dy, at(dk=1))

    act_first = slots(16)
    act_sib = slots(16)

    def act_shard(dzh, dx):
        index = ((zh - dzh) % 4) * 8 + ((x - dx) % 4) * 2 + core
        return act.at[pl.ds(pl.multiple_of(index * 64, 64), 64)]

    def act_from_sibling(dzh, dx):
        index = ((zh - dzh) % 4) * 8 + ((x - dx) % 4) * 2 + sib
        return act.at[pl.ds(pl.multiple_of(index * 64, 64), 64)]

    def act_along_x(dzh):
        for dx in (1, 3, 2):
            send(act_shard(dzh, 0), act_shard(dzh, 0), act_first + dzh * 4 + dx, at(dx=dx))
        act_to_sibling(dzh, 0)

    def act_to_sibling(dzh, dx):
        send(act_shard(dzh, dx), act_shard(dzh, dx), act_sib + dzh * 4 + dx, at(dk=1))

    act_z = {
        dzh: copy(act_shard(0, 0), act_shard(0, 0), act_first + dzh * 4, at(dzh=dzh))
        for dzh in (1, 3, 2)
    }
    sends.extend(act_z.values())

    for key in links:
        answer(key)
    for dzh in (1, 3, 2):
        @pl.when(jnp.logical_not(links["z", dzh][0]))
        def _(dzh=dzh):
            act_z[dzh].start()

    def act_z_later(pairs):
        for dzh in (1, 3, 2):
            first, _, _, slot = links["z", dzh]
            farthest = (zh == 0) & (dzh == 2)

            @pl.when(first & (farthest if pairs == "far" else jnp.logical_not(farthest)))
            def _(dzh=dzh, slot=slot):
                pl.semaphore_wait(ready_sem.at[slot], 1)
                act_z[dzh].start()

    for item in loads[3:]:
        item.wait()
    row_ids = lax.broadcasted_iota(jnp.int32, (2 * SHARD, CHUNK), 0) % SHARD + ctx * SHARD
    pick = (
        lax.broadcasted_iota(jnp.int32, (2 * SHARD, 32), 1)
        == (lax.broadcasted_iota(jnp.int32, (2 * SHARD, 32), 0) % SHARD + ctx * SHARD) // BLK
    )
    mask_rows = dot(pick.astype(BF16), mask_in[...].astype(BF16)).astype(BF16)

    def bias_step(step, carry):
        cols = pl.ds(pl.multiple_of(step * CHUNK, CHUNK), CHUNK)
        col_ids = lax.broadcasted_iota(jnp.int32, (2 * SHARD, CHUNK), 1) + step * CHUNK
        spread = (
            (lax.broadcasted_iota(jnp.int32, (32, CHUNK), 1) + step * CHUNK) // BLK
            == lax.broadcasted_iota(jnp.int32, (32, CHUNK), 0)
        )
        wide = dot(mask_rows, spread.astype(BF16))
        bias[:, cols] = jnp.where((wide > 0.5) & (col_ids <= row_ids), 0.0, NEG)
        return carry

    lax.fori_loop(0, TOK // CHUNK, bias_step, 0)
    query = stacked(query_in[...])
    grad = stacked(grad_in[...])
    delta = jnp.sum(grad.astype(F32) * stacked(out_in[...]).astype(F32), axis=1, keepdims=True)

    def block_scores(dz, dy):
        index = ((z - dz) % 4) * 4 + (y - dy) % 4
        if dz or dy:
            arrive(kv_all.at[sib, rows_of(index)], sib_first + dz * 4 + dy)
        cols = pl.ds(pl.multiple_of(index * SHARD, SHARD), SHARD)
        part = dot_t(query, kv_all[0, rows_of(index), :]) + bias[:, cols]
        scores[:, cols] = part
        slopes[:, cols] = dot_t(grad, kv_all[1, rows_of(index), :])
        top[...] = jnp.maximum(top[...], part) if dz or dy else part

    block_scores(0, 0)

    for dz in (1, 3, 2):
        kv_gather.wait(dz, 0)
        kv_gather.along_y(dz)
        to_sibling(dz, 0)
    for dx in (1, 3, 2):
        await_answer(("x", dx))
    act_along_x(0)

    waiting = [(1, 0), (3, 0), (2, 0)]
    for dz in (0, 1, 3, 2):
        for dy in (1, 3, 2):
            kv_gather.wait(dz, dy)
            to_sibling(dz, dy)
            waiting.append((dz, dy))
            if len(waiting) > 2:
                block_scores(*waiting.pop(0))
        if dz == 1:
            act_z_later("near")
    for block in waiting:
        block_scores(*block)

    scale = HD ** -0.5
    power = scale * 1.4426950408889634
    row_max = jnp.max(top[...], axis=1, keepdims=True)

    def prob_step(step, total):
        cols = pl.ds(pl.multiple_of(step * CHUNK, CHUNK), CHUNK)
        part = jnp.exp2((scores[:, cols] - row_max) * power)
        probs[:, cols] = part.astype(BF16)
        dsc[:, cols] = (part * (slopes[:, cols] - delta)).astype(BF16)
        return total + part[:, :HD] + part[:, HD:]

    total = lax.fori_loop(0, TOK // CHUNK, prob_step, jnp.zeros((2 * SHARD, HD), F32))
    inverse = 1.0 / jnp.sum(total, axis=1, keepdims=True)

    def mine_first(value):
        turned = value.T
        low, high = turned[:64], turned[64:]
        return jnp.concatenate(
            [jnp.where(core == 0, low, high), jnp.where(core == 0, high, low)], axis=0
        ).astype(BF16)

    query_t = mine_first(query.astype(F32) * (inverse * scale))
    grad_t = mine_first(grad.astype(F32) * inverse)

    core_slot = slots(4)
    y_slot = slots(4)

    def terms(dy):
        def term_step(step, carry):
            index = step * 4 + (y + dy) % 4
            cols = pl.ds(pl.multiple_of(index * SHARD, SHARD), SHARD)
            key_part = dot(query_t, dsc[:, cols])
            value_part = dot(grad_t, probs[:, cols])
            own[dy, step, 0] = key_part[:64]
            own[dy, step, 1] = value_part[:64]
            sib_send[dy, step, 0] = key_part[64:].astype(BF16)
            sib_send[dy, step, 1] = value_part[64:].astype(BF16)
            return carry

        lax.fori_loop(0, 4, term_step, 0)
        send(sib_send.at[dy], sib_recv.at[dy], core_slot + dy, at(dk=1))

    def to_y(dy):
        arrive(sib_recv.at[dy], core_slot + dy)
        y_send[dy - 1] = (own[dy] + sib_recv[dy].astype(F32)).astype(BF16)
        send(y_send.at[dy - 1], y_recv.at[dy - 1], y_slot + dy, at(dy=dy))

    terms(2)
    terms(1)
    to_y(2)
    terms(3)
    to_y(1)
    terms(0)
    to_y(3)
    act_z_later("far")

    query_grad = dot(dsc[...], kv_all[0]) * (inverse * scale)
    q_out[:, :HD] = query_grad[:SHARD].astype(BF16)
    q_out[:, HD:] = query_grad[SHARD:].astype(BF16)
    own_lanes = pl.ds(pl.multiple_of(ctx * SHARD, SHARD), SHARD)
    q_all[:HD, own_lanes] = query_grad[:SHARD].T.astype(BF16)
    q_all[HD:, own_lanes] = query_grad[SHARD:].T.astype(BF16)

    def lanes_of(index):
        return pl.ds(pl.multiple_of(index * SHARD, SHARD), SHARD)

    q_gather = Gather(lambda index: q_all.at[:, lanes_of(index)])
    q_gather.start()

    for dzh in (1, 3):
        arrive(act_shard(dzh, 0), act_first + dzh * 4)
        act_along_x(dzh)

    arrive(sib_recv.at[0], core_slot)
    for dy in (1, 3, 2):
        arrive(y_recv.at[dy - 1], y_slot + dy)
    y_sum = own[0] + sib_recv[0].astype(F32)
    for dy in (1, 2, 3):
        y_sum = y_sum + y_recv[dy - 1].astype(F32)
    own[0] = y_sum
    zx_send[...] = y_sum.astype(BF16)

    zx_slot = slots(8)
    for dz in (1, 2, 3):
        await_answer(("f", dz))
    for dz in (1, 3, 2, 0):
        for dx in (0, 1):
            if dz or dx:
                part = side if dx == 0 else 1 - side
                slot = dz * 2 + dx
                send(
                    zx_send.at[(z + dz) % 4, part], zx_recv.at[slot], zx_slot + slot,
                    flip(dz) if dx else at(dz=dz),
                )

    for dz in (1, 3, 2):
        q_gather.wait(dz, 0)
        q_gather.along_y(dz)
    arrive(act_shard(2, 0), act_first + 8)
    act_along_x(2)

    kv_sum = own[0, z, side]
    for slot in range(1, 8):
        arrive(zx_recv.at[slot], zx_slot + slot)
    for slot in range(1, 8):
        kv_sum = kv_sum + zx_recv[slot].astype(F32)
    g_all[:, own_lanes] = kv_sum.astype(BF16)
    g_gather = Gather(lambda index: g_all.at[:, lanes_of(index)])
    g_gather.start()
    kv_out[...] = kv_sum.astype(BF16)

    for dzh in (0, 1, 3):
        for dx in (1, 3, 2):
            arrive(act_shard(dzh, dx), act_first + dzh * 4 + dx)
            act_to_sibling(dzh, dx)

    for dz in (1, 3, 2):
        g_gather.wait(dz, 0)
        g_gather.along_y(dz)

    for dx in (1, 3, 2):
        arrive(act_shard(2, dx), act_first + 8 + dx)
        act_to_sibling(2, dx)
    for dz in range(4):
        for dy in (1, 3, 2):
            q_gather.wait(dz, dy)
    for dzh in range(4):
        for dx in range(4):
            arrive(act_from_sibling(dzh, dx), act_sib + dzh * 4 + dx)
    wq_out[...] = dot(q_all[...], act[...]).T.astype(BF16)

    for dz in range(4):
        for dy in (1, 3, 2):
            g_gather.wait(dz, dy)
    wkv_out[...] = dot(g_all[...], act[...]).astype(BF16)

    for item in sends:
        item.wait_send()


def deliver(*refs):
    for source, result in zip(refs[:4], refs[4:]):
        result[...] = source[...]


def per_device(inputs, queries, keys, values, outputs, out_grad, block_mask):
    vmem = pl.BlockSpec(memory_space=pltpu.VMEM)
    anywhere = pl.BlockSpec(memory_space=pl.ANY)
    shapes = (
        jax.ShapeDtypeStruct((SHARD, 256), BF16),
        jax.ShapeDtypeStruct((64, SHARD), BF16),
        jax.ShapeDtypeStruct((512, 256), BF16),
        jax.ShapeDtypeStruct((64, 512), BF16),
    )
    results = pl.pallas_call(
        body,
        name="attention_backward",
        out_shape=shapes,
        in_specs=[anywhere] * 7,
        out_specs=(vmem, vmem, vmem, vmem),
        scratch_shapes=[
            pltpu.VMEM((SHARD, 256), BF16),
            pltpu.VMEM((SHARD, 256), BF16),
            pltpu.VMEM((SHARD, 256), BF16),
            pltpu.VMEM((32, 32), jnp.int32),
            pltpu.VMEM((TOK, 512), BF16),
            pltpu.VMEM((2, TOK, HD), BF16),
            pltpu.VMEM((256, TOK), BF16),
            pltpu.VMEM((64, TOK), BF16),
            pltpu.VMEM((256, TOK), F32),
            pltpu.VMEM((256, TOK), F32),
            pltpu.VMEM((256, TOK), BF16),
            pltpu.VMEM((256, TOK), BF16),
            pltpu.VMEM((256, TOK), F32),
            pltpu.VMEM((256, HD), F32),
            pltpu.VMEM((4, 4, 2, 64, HD), BF16),
            pltpu.VMEM((4, 4, 2, 64, HD), BF16),
            pltpu.VMEM((4, 4, 2, 64, HD), F32),
            pltpu.VMEM((3, 4, 2, 64, HD), BF16),
            pltpu.VMEM((3, 4, 2, 64, HD), BF16),
            pltpu.VMEM((4, 2, 64, HD), BF16),
            pltpu.VMEM((8, 64, HD), BF16),
            pltpu.SemaphoreType.DMA((128,)),
            pltpu.SemaphoreType.DMA((128,)),
            pltpu.SemaphoreType.DMA((7,)),
            pltpu.SemaphoreType.REGULAR((12,)),
        ],
        compiler_params=pltpu.CompilerParams(
            collective_id=0, has_side_effects=True, vmem_limit_bytes=VMEM_LIMIT
        ),
        cost_estimate=pl.CostEstimate(
            flops=1_400_000_000, bytes_accessed=4 << 20, transcendentals=256 * TOK
        ),
    )(inputs, queries, keys, values, outputs, out_grad, block_mask)
    q_grad, kv_turned, weight_q, weight_kv_turned = pl.pallas_call(
        deliver,
        name="deliver",
        out_shape=shapes,
        in_specs=[vmem] * 4,
        out_specs=[vmem] * 4,
        compiler_params=pltpu.CompilerParams(vmem_limit_bytes=VMEM_LIMIT),
    )(*results)
    return q_grad, kv_turned.T, weight_q, weight_kv_turned.T


def solution(mesh):
    in_specs = (
        P("head", "ctx"),
        P("ctx", "head"),
        P("ctx", None),
        P("ctx", None),
        P("ctx", "head"),
        P("ctx", "head"),
        P(),
    )
    out_specs = (P("ctx", "head"), P("ctx", "head"), P("ctx", "head"), P("ctx", "head"))
    return jax.shard_map(
        per_device, mesh=mesh, in_specs=in_specs, out_specs=out_specs, check_vma=False
    )
```

```python
import functools

import jax
import jax.numpy as jnp
from jax import lax
from jax.experimental import pallas as pl
from jax.experimental.pallas import tpu as pltpu
from jax.sharding import PartitionSpec as P

HD = 128
BLK = 64
TOK = 2048
SHARD = 128
SPAN = 512
MESH = pl.DeviceIdType.MESH
NEG = -1e30
VMEM_LIMIT = 60 << 20
F32 = jnp.float32
BF16 = jnp.bfloat16

def dot(left, right):
    return lax.dot_general(left, right, (((1,), (0,)), ((), ())), preferred_element_type=F32)


def dot_t(left, right):
    return lax.dot_general(left, right, (((1,), (1,)), ((), ())), preferred_element_type=F32)


def stacked(value):
    return jnp.concatenate([value[:, :HD], value[:, HD:]], axis=0)


def body(
    inputs, queries, keys, values, outputs, out_grad, block_mask,
    q_out, kv_out, wq_out, wkv_out,
    query_in, grad_in, out_in, mask_in,
    act, kv_all, q_all, g_all, scores, slopes, probs, dsc, bias, top, query_turned, grad_turned,
    sib_send, sib_recv, own, y_send, y_recv, zx_send, zx_recv,
    send_sem, recv_sem, local_sem, ready_sem,
):
    ctx = lax.axis_index("ctx")
    head = lax.axis_index("head")
    z, y = ctx // 4, ctx % 4
    zh, x, core = head // 8, (head // 2) % 4, head % 2
    sib = 1 - core
    side = x % 2
    group = head // 4

    def at(dz=0, dy=0, dzh=0, dx=0, dk=0):
        return (
            ((z + dz) % 4) * 4 + (y + dy) % 4,
            ((zh + dzh) % 4) * 8 + ((x + dx) % 4) * 2 + (core + dk) % 2,
        )

    def flip(dz):
        return (((z + dz) % 4) * 4 + y, zh * 8 + (x + 1 - 2 * side) * 2 + core)

    counter = [0]
    sends = []

    def slots(count):
        first = counter[0]
        counter[0] += count
        return first

    def copy(src, dst, slot, device):
        return pltpu.make_async_remote_copy(
            src_ref=src, dst_ref=dst, send_sem=send_sem.at[slot], recv_sem=recv_sem.at[slot],
            device_id=device, device_id_type=MESH,
        )

    def send(src, dst, slot, device):
        item = copy(src, dst, slot, device)
        item.start()
        sends.append(item)

    def arrive(dst, slot):
        copy(dst, dst, slot, at(dk=1)).wait_recv()

    def signal(sem, device):
        pl.semaphore_signal(sem, inc=1, device_id=device, device_id_type=MESH)

    def place_of(dz, dy):
        return pl.ds(pl.multiple_of((((y - dy) % 4) * 4 + (z - dz) % 4) * SHARD, SHARD), SHARD)

    own_rows = place_of(0, 0)
    own_cols = pl.ds(pl.multiple_of(group * HD, HD), HD)
    own_act = pl.ds(pl.multiple_of(head * 64, 64), 64)
    loads = [
        pltpu.make_async_copy(keys.at[:, own_cols], kv_all.at[0, own_rows], local_sem.at[0]),
        pltpu.make_async_copy(values.at[:, own_cols], kv_all.at[1, own_rows], local_sem.at[1]),
        pltpu.make_async_copy(inputs, act.at[own_act], local_sem.at[2]),
        pltpu.make_async_copy(block_mask, mask_in, local_sem.at[3]),
        pltpu.make_async_copy(queries, query_in, local_sem.at[4]),
        pltpu.make_async_copy(out_grad, grad_in, local_sem.at[5]),
        pltpu.make_async_copy(outputs, out_in, local_sem.at[6]),
    ]
    for item in loads:
        item.start()

    def rank_of(index):
        return jnp.where(index < 2, index, 5 - index)

    barrier = pltpu.get_barrier_semaphore()
    for offset in (1, 2, 3):
        signal(barrier, at(dy=offset))
        signal(barrier, at(dz=offset))
    signal(barrier, at(dk=1))

    rank_z, rank_x = rank_of(zh), rank_of(x)
    pair_first = (x == 0) | (x == 3)
    links = {}
    for offset in (1, 2, 3):
        links["z", offset] = (
            rank_z < rank_of((zh + offset) % 4), at(dzh=offset), offset, 4 - offset
        )
        links["x", offset] = (
            rank_x < rank_of((x + offset) % 4), at(dx=offset), 4 + offset, 8 - offset
        )
        links["f", offset] = (pair_first, flip(offset), 8 + offset, 12 - offset)

    for first, device, _, _ in links.values():
        @pl.when(first)
        def _(device=device):
            signal(barrier, device)

    for item in loads[:3]:
        item.wait()
    pl.semaphore_wait(barrier, 7 + rank_z + rank_x + jnp.where(pair_first, 0, 3))

    def answer(key):
        first, device, slot, _ = links[key]

        @pl.when(jnp.logical_not(first))
        def _():
            signal(ready_sem.at[slot], device)

    def await_answer(key):
        first, _, _, slot = links[key]

        @pl.when(first)
        def _():
            pl.semaphore_wait(ready_sem.at[slot], 1)

    class Gather:
        def __init__(self, shard):
            self.shard = shard
            self.first = slots(16)

        def start(self):
            for dz in (1, 3, 2):
                send(self.shard(0, 0), self.shard(0, 0), self.first + dz * 4, at(dz=dz))
            self.along_y(0)

        def along_y(self, dz):
            for dy in (1, 3, 2):
                send(self.shard(dz, 0), self.shard(dz, 0), self.first + dz * 4 + dy, at(dy=dy))

        def wait(self, dz, dy):
            arrive(self.shard(dz, dy), self.first + dz * 4 + dy)

    kv_gather = Gather(lambda dz, dy: kv_all.at[core, place_of(dz, dy)])
    kv_gather.start()
    sib_first = slots(16)

    def to_sibling(dz, dy):
        part = kv_gather.shard(dz, dy)
        send(part, part, sib_first + dz * 4 + dy, at(dk=1))

    act_first = slots(16)
    act_sib = slots(16)

    def act_shard(dzh, dx):
        index = ((zh - dzh) % 4) * 8 + ((x - dx) % 4) * 2 + core
        return act.at[pl.ds(pl.multiple_of(index * 64, 64), 64)]

    def act_from_sibling(dzh, dx):
        index = ((zh - dzh) % 4) * 8 + ((x - dx) % 4) * 2 + sib
        return act.at[pl.ds(pl.multiple_of(index * 64, 64), 64)]

    def act_along_x(dzh):
        for dx in (1, 3, 2):
            send(act_shard(dzh, 0), act_shard(dzh, 0), act_first + dzh * 4 + dx, at(dx=dx))
        act_to_sibling(dzh, 0)

    def act_to_sibling(dzh, dx):
        send(act_shard(dzh, dx), act_shard(dzh, dx), act_sib + dzh * 4 + dx, at(dk=1))

    act_z = {
        dzh: copy(act_shard(0, 0), act_shard(0, 0), act_first + dzh * 4, at(dzh=dzh))
        for dzh in (1, 3, 2)
    }
    sends.extend(act_z.values())

    for key in links:
        answer(key)
    def act_z_lower(to_first):
        for dzh in (1, 3, 2):
            first_rank = (zh + dzh) % 4 == 0
            chosen = first_rank if to_first else jnp.logical_not(first_rank)

            @pl.when(jnp.logical_not(links["z", dzh][0]) & chosen)
            def _(dzh=dzh):
                act_z[dzh].start()

    act_z_lower(True)

    def act_z_later(pairs):
        for dzh in (1, 3, 2):
            first, _, _, slot = links["z", dzh]
            farthest = (zh == 0) & (dzh == 2)

            @pl.when(first & (farthest if pairs == "far" else jnp.logical_not(farthest)))
            def _(dzh=dzh, slot=slot):
                pl.semaphore_wait(ready_sem.at[slot], 1)
                act_z[dzh].start()

    for item in loads[3:]:
        item.wait()
    row_ids = lax.broadcasted_iota(jnp.int32, (2 * SHARD, SHARD), 0) % SHARD + ctx * SHARD
    pick = (
        lax.broadcasted_iota(jnp.int32, (2 * SHARD, 32), 1)
        == (lax.broadcasted_iota(jnp.int32, (2 * SHARD, 32), 0) % SHARD + ctx * SHARD) // BLK
    )
    mask_rows = dot(pick.astype(BF16), mask_in[...].astype(BF16)).astype(BF16)

    def bias_step(step, carry):
        cols = pl.ds(pl.multiple_of(step * SHARD, SHARD), SHARD)
        first = ((step % 4) * 4 + step // 4) * SHARD
        col_ids = lax.broadcasted_iota(jnp.int32, (2 * SHARD, SHARD), 1) + first
        spread = (
            (lax.broadcasted_iota(jnp.int32, (32, SHARD), 1) + first) // BLK
            == lax.broadcasted_iota(jnp.int32, (32, SHARD), 0)
        )
        wide = dot(mask_rows, spread.astype(BF16))
        bias[:, cols] = jnp.where((wide > 0.5) & (col_ids <= row_ids), 0.0, NEG)
        return carry

    lax.fori_loop(0, TOK // SHARD, bias_step, 0, unroll=2)
    query = stacked(query_in[...])
    grad = stacked(grad_in[...])
    delta = jnp.sum(grad.astype(F32) * stacked(out_in[...]).astype(F32), axis=1, keepdims=True)

    def mine_first(value):
        turned = value.astype(F32).T
        low, high = turned[:64], turned[64:]
        return jnp.concatenate(
            [jnp.where(core == 0, low, high), jnp.where(core == 0, high, low)], axis=0
        )

    query_turned[...] = mine_first(query)
    grad_turned[...] = mine_first(grad)

    def block_scores(dz, dy):
        span = place_of(dz, dy)
        if dz or dy:
            arrive(kv_all.at[sib, span], sib_first + dz * 4 + dy)
        part = dot_t(query, kv_all[0, span, :]) + bias[:, span]
        scores[:, span] = part
        slopes[:, span] = dot_t(grad, kv_all[1, span, :])
        top[...] = jnp.maximum(top[...], part) if dz or dy else part

    block_scores(0, 0)

    for dz in (1, 3, 2):
        kv_gather.wait(dz, 0)
        kv_gather.along_y(dz)
        to_sibling(dz, 0)
    act_z_lower(False)
    for dx in (1, 3, 2):
        await_answer(("x", dx))
    act_along_x(0)

    waiting = [(1, 0), (3, 0), (2, 0)]
    for dz in (0, 1, 3, 2):
        for dy in (1, 3, 2):
            kv_gather.wait(dz, dy)
            to_sibling(dz, dy)
            waiting.append((dz, dy))
            if len(waiting) > 2:
                block_scores(*waiting.pop(0))
        if dz == 1:
            act_z_later("near")
    for block in waiting:
        block_scores(*block)

    scale = HD ** -0.5
    power = scale * 1.4426950408889634
    row_max = jnp.max(top[...], axis=1, keepdims=True)
    total = jnp.zeros((2 * SHARD, HD), F32)
    for step in range(TOK // SPAN):
        cols = slice(step * SPAN, (step + 1) * SPAN)
        part = jnp.exp2((scores[:, cols] - row_max) * power)
        scores[:, cols] = part
        probs[:, cols] = part.astype(BF16)
        for lane in range(0, SPAN, HD):
            total = total + part[:, lane : lane + HD]
    inverse_row = 1.0 / jnp.sum(total.T, axis=0, keepdims=True)
    query_t = (query_turned[...] * (inverse_row * scale)).astype(BF16)
    grad_t = (grad_turned[...] * inverse_row).astype(BF16)

    core_slot = slots(8)
    y_slot = slots(8)

    def span_of(dy):
        return pl.ds(pl.multiple_of(((y + dy) % 4) * SPAN, SPAN), SPAN)

    def terms(part, dy):
        span = span_of(dy)
        if part:
            result = dot(grad_t, probs[:, span])
        else:
            slope = (scores[:, span] * (slopes[:, span] - delta)).astype(BF16)
            dsc[:, span] = slope
            result = dot(query_t, slope)
        for step in range(4):
            lanes = slice(step * SHARD, (step + 1) * SHARD)
            own[part, dy, step] = result[:64, lanes]
            sib_send[part, dy, step] = result[64:, lanes].astype(BF16)
        send(sib_send.at[part, dy], sib_recv.at[part, dy], core_slot + part * 4 + dy, at(dk=1))

    def to_y(part, dy):
        arrive(sib_recv.at[part, dy], core_slot + part * 4 + dy)
        y_send[part, dy - 1] = (own[part, dy] + sib_recv[part, dy].astype(F32)).astype(BF16)
        send(
            y_send.at[part, dy - 1], y_recv.at[part, dy - 1], y_slot + part * 4 + dy, at(dy=dy)
        )

    for dy in (2, 1, 3, 0):
        terms(1, dy)
    terms(0, 2)
    to_y(1, 2)
    to_y(1, 1)
    terms(0, 1)
    to_y(1, 3)
    terms(0, 3)
    to_y(0, 2)
    terms(0, 0)
    to_y(0, 1)
    to_y(0, 3)
    act_z_later("far")

    inverse = 1.0 / jnp.sum(total, axis=1, keepdims=True)
    query_grad = dot(dsc[...], kv_all[0]) * (inverse * scale)
    q_out[:, :HD] = query_grad[:SHARD].astype(BF16)
    q_out[:, HD:] = query_grad[SHARD:].astype(BF16)
    own_lanes = pl.ds(pl.multiple_of(ctx * SHARD, SHARD), SHARD)
    q_all[:HD, own_lanes] = query_grad[:SHARD].T.astype(BF16)
    q_all[HD:, own_lanes] = query_grad[SHARD:].T.astype(BF16)

    def lanes_of(dz, dy):
        index = ((z - dz) % 4) * 4 + (y - dy) % 4
        return pl.ds(pl.multiple_of(index * SHARD, SHARD), SHARD)

    q_gather = Gather(lambda dz, dy: q_all.at[:, lanes_of(dz, dy)])
    q_gather.start()

    for dzh in (1, 3):
        arrive(act_shard(dzh, 0), act_first + dzh * 4)
        act_along_x(dzh)

    zx_slot = slots(8)

    def to_zx(part):
        arrive(sib_recv.at[part, 0], core_slot + part * 4)
        for dy in (1, 3, 2):
            arrive(y_recv.at[part, dy - 1], y_slot + part * 4 + dy)
        y_sum = own[part, 0] + sib_recv[part, 0].astype(F32)
        for dy in (1, 2, 3):
            y_sum = y_sum + y_recv[part, dy - 1].astype(F32)
        own[part, 0] = y_sum
        zx_send[part] = y_sum.astype(BF16)
        other = jnp.where(side == part, 0, 1)
        for dz in (1, 3, 2):
            slot = dz * 2 + other
            device = (((z + dz) % 4) * 4 + y, zh * 8 + (x - side + part) * 2 + core)
            send(zx_send.at[part, (z + dz) % 4], zx_recv.at[slot], zx_slot + slot, device)

        @pl.when(side != part)
        def _():
            copy(zx_send.at[part, z], zx_recv.at[1], zx_slot + 1, flip(0)).start()

    for dz in (1, 2, 3):
        await_answer(("f", dz))
    to_zx(1)
    to_zx(0)
    sends.append(copy(zx_send.at[0, 0], zx_recv.at[1], zx_slot + 1, flip(0)))

    for dz in (1, 3, 2):
        q_gather.wait(dz, 0)
        q_gather.along_y(dz)
    arrive(act_shard(2, 0), act_first + 8)
    act_along_x(2)

    kv_sum = own[side, 0, z]
    for slot in range(1, 8):
        arrive(zx_recv.at[slot], zx_slot + slot)
    for slot in range(1, 8):
        kv_sum = kv_sum + zx_recv[slot].astype(F32)
    g_all[:, own_lanes] = kv_sum.astype(BF16)
    g_gather = Gather(lambda dz, dy: g_all.at[:, lanes_of(dz, dy)])
    g_gather.start()
    kv_out[...] = kv_sum.astype(BF16)

    for dzh in (0, 1, 3):
        for dx in (1, 3, 2):
            arrive(act_shard(dzh, dx), act_first + dzh * 4 + dx)
            act_to_sibling(dzh, dx)

    for dz in (1, 3, 2):
        g_gather.wait(dz, 0)
        g_gather.along_y(dz)

    for dx in (1, 3, 2):
        arrive(act_shard(2, dx), act_first + 8 + dx)
        act_to_sibling(2, dx)
    for dz in range(4):
        for dy in (1, 3, 2):
            q_gather.wait(dz, dy)
    for dzh in range(4):
        for dx in range(4):
            arrive(act_from_sibling(dzh, dx), act_sib + dzh * 4 + dx)
    wq_out[...] = dot(q_all[...], act[...]).T.astype(BF16)

    for dz in range(4):
        for dy in (1, 3, 2):
            g_gather.wait(dz, dy)
    wkv_out[...] = dot(g_all[...], act[...]).astype(BF16)

    for item in sends:
        item.wait_send()


def deliver(*refs):
    sources, results, sem = refs[:4], refs[4:8], refs[8]
    items = [
        pltpu.make_async_copy(source, result, sem.at[index])
        for index, (source, result) in enumerate(zip(sources, results))
    ]
    for item in items:
        item.start()
    for item in items:
        item.wait()


def per_device(inputs, queries, keys, values, outputs, out_grad, block_mask):
    vmem = pl.BlockSpec(memory_space=pltpu.VMEM)
    anywhere = pl.BlockSpec(memory_space=pl.ANY)
    shapes = (
        jax.ShapeDtypeStruct((SHARD, 256), BF16),
        jax.ShapeDtypeStruct((64, SHARD), BF16),
        jax.ShapeDtypeStruct((512, 256), BF16),
        jax.ShapeDtypeStruct((64, 512), BF16),
    )
    results = pl.pallas_call(
        body,
        name="attention_backward",
        out_shape=tuple(pltpu.VMEM(shape.shape, shape.dtype) for shape in shapes),
        in_specs=[anywhere] * 7,
        out_specs=(vmem, vmem, vmem, vmem),
        scratch_shapes=[
            pltpu.VMEM((SHARD, 256), BF16),
            pltpu.VMEM((SHARD, 256), BF16),
            pltpu.VMEM((SHARD, 256), BF16),
            pltpu.VMEM((32, 32), jnp.int32),
            pltpu.VMEM((TOK, 512), BF16),
            pltpu.VMEM((2, TOK, HD), BF16),
            pltpu.VMEM((256, TOK), BF16),
            pltpu.VMEM((64, TOK), BF16),
            pltpu.VMEM((256, TOK), F32),
            pltpu.VMEM((256, TOK), F32),
            pltpu.VMEM((256, TOK), BF16),
            pltpu.VMEM((256, TOK), BF16),
            pltpu.VMEM((256, TOK), F32),
            pltpu.VMEM((256, HD), F32),
            pltpu.VMEM((HD, 256), F32),
            pltpu.VMEM((HD, 256), F32),
            pltpu.VMEM((2, 4, 4, 64, HD), BF16),
            pltpu.VMEM((2, 4, 4, 64, HD), BF16),
            pltpu.VMEM((2, 4, 4, 64, HD), F32),
            pltpu.VMEM((2, 3, 4, 64, HD), BF16),
            pltpu.VMEM((2, 3, 4, 64, HD), BF16),
            pltpu.VMEM((2, 4, 64, HD), BF16),
            pltpu.VMEM((8, 64, HD), BF16),
            pltpu.SemaphoreType.DMA((128,)),
            pltpu.SemaphoreType.DMA((128,)),
            pltpu.SemaphoreType.DMA((7,)),
            pltpu.SemaphoreType.REGULAR((12,)),
        ],
        compiler_params=pltpu.CompilerParams(
            collective_id=0, has_side_effects=True, vmem_limit_bytes=VMEM_LIMIT
        ),
        cost_estimate=pl.CostEstimate(
            flops=1_400_000_000, bytes_accessed=4 << 20, transcendentals=256 * TOK
        ),
    )(inputs, queries, keys, values, outputs, out_grad, block_mask)
    q_grad, kv_turned, weight_q, weight_kv_turned = pl.pallas_call(
        deliver,
        name="deliver",
        out_shape=shapes,
        in_specs=[vmem] * 4,
        out_specs=[anywhere] * 4,
        scratch_shapes=[pltpu.SemaphoreType.DMA((4,))],
        compiler_params=pltpu.CompilerParams(vmem_limit_bytes=4 << 20),
    )(*results)
    return q_grad, kv_turned.T, weight_q, weight_kv_turned.T


def solution(mesh):
    in_specs = (
        P("head", "ctx"),
        P("ctx", "head"),
        P("ctx", None),
        P("ctx", None),
        P("ctx", "head"),
        P("ctx", "head"),
        P(),
    )
    out_specs = (P("ctx", "head"), P("ctx", "head"), P("ctx", "head"), P("ctx", "head"))
    return jax.shard_map(
        per_device, mesh=mesh, in_specs=in_specs, out_specs=out_specs, check_vma=False
    )
```

```python
import functools

import jax
import jax.numpy as jnp
from jax import lax
from jax.experimental import pallas as pl
from jax.experimental.pallas import tpu as pltpu
from jax.sharding import PartitionSpec as P

HD = 128
BLK = 64
TOK = 2048
SHARD = 128
SPAN = 512
RELAYED = (0, 1, 3)
MESH = pl.DeviceIdType.MESH
NEG = -1e30
VMEM_LIMIT = 60 << 20
F32 = jnp.float32
BF16 = jnp.bfloat16

def dot(left, right):
    return lax.dot_general(left, right, (((1,), (0,)), ((), ())), preferred_element_type=F32)


def dot_t(left, right):
    return lax.dot_general(left, right, (((1,), (1,)), ((), ())), preferred_element_type=F32)


def stacked(value):
    return jnp.concatenate([value[:, :HD], value[:, HD:]], axis=0)


def body(
    inputs, queries, keys, values, outputs, out_grad, block_mask,
    q_out, kv_out, wq_out, wkv_out,
    query_in, grad_in, out_in, mask_in,
    act, kv_all, q_all, g_all, scores, slopes, probs, dsc, bias, top, query_turned, grad_turned,
    sib_send, sib_recv, own, y_send, y_recv, zx_send, zx_recv,
    send_sem, recv_sem, local_sem, ready_sem,
):
    ctx = lax.axis_index("ctx")
    head = lax.axis_index("head")
    z, y = ctx // 4, ctx % 4
    zh, x, core = head // 8, (head // 2) % 4, head % 2
    sib = 1 - core
    side = x % 2
    group = head // 4

    def at(dz=0, dy=0, dzh=0, dx=0, dk=0):
        return (
            ((z + dz) % 4) * 4 + (y + dy) % 4,
            ((zh + dzh) % 4) * 8 + ((x + dx) % 4) * 2 + (core + dk) % 2,
        )

    def flip(dz):
        return (((z + dz) % 4) * 4 + y, zh * 8 + (x + 1 - 2 * side) * 2 + core)

    counter = [0]
    sends = []

    def slots(count):
        first = counter[0]
        counter[0] += count
        return first

    def copy(src, dst, slot, device):
        return pltpu.make_async_remote_copy(
            src_ref=src, dst_ref=dst, send_sem=send_sem.at[slot], recv_sem=recv_sem.at[slot],
            device_id=device, device_id_type=MESH,
        )

    def send(src, dst, slot, device):
        item = copy(src, dst, slot, device)
        item.start()
        sends.append(item)

    def arrive(dst, slot):
        copy(dst, dst, slot, at(dk=1)).wait_recv()

    def signal(sem, device):
        pl.semaphore_signal(sem, inc=1, device_id=device, device_id_type=MESH)

    def place_of(dz, dy):
        return pl.ds(pl.multiple_of((((y - dy) % 4) * 4 + (z - dz) % 4) * SHARD, SHARD), SHARD)

    own_rows = place_of(0, 0)
    own_cols = pl.ds(pl.multiple_of(group * HD, HD), HD)
    own_act = pl.ds(pl.multiple_of(head * 64, 64), 64)
    loads = [
        pltpu.make_async_copy(keys.at[:, own_cols], kv_all.at[0, own_rows], local_sem.at[0]),
        pltpu.make_async_copy(values.at[:, own_cols], kv_all.at[1, own_rows], local_sem.at[1]),
        pltpu.make_async_copy(inputs, act.at[own_act], local_sem.at[2]),
        pltpu.make_async_copy(block_mask, mask_in, local_sem.at[3]),
        pltpu.make_async_copy(queries, query_in, local_sem.at[4]),
        pltpu.make_async_copy(out_grad, grad_in, local_sem.at[5]),
        pltpu.make_async_copy(outputs, out_in, local_sem.at[6]),
    ]
    for item in loads:
        item.start()

    def rank_of(index):
        return jnp.where(index < 2, index, 5 - index)

    barrier = pltpu.get_barrier_semaphore()
    for offset in (1, 2, 3):
        signal(barrier, at(dy=offset))
        signal(barrier, at(dz=offset))
    signal(barrier, at(dk=1))

    rank_z, rank_x = rank_of(zh), rank_of(x)
    pair_first = (x == 0) | (x == 3)
    links = {}
    for offset in (1, 2, 3):
        links["z", offset] = (
            rank_z < rank_of((zh + offset) % 4), at(dzh=offset), offset, 4 - offset
        )
        links["x", offset] = (
            rank_x < rank_of((x + offset) % 4), at(dx=offset), 4 + offset, 8 - offset
        )
        links["f", offset] = (pair_first, flip(offset), 8 + offset, 12 - offset)

    for first, device, _, _ in links.values():
        @pl.when(first)
        def _(device=device):
            signal(barrier, device)

    for item in loads[:3]:
        item.wait()
    pl.semaphore_wait(barrier, 7 + rank_z + rank_x + jnp.where(pair_first, 0, 3))

    def answer(key):
        first, device, slot, _ = links[key]

        @pl.when(jnp.logical_not(first))
        def _():
            signal(ready_sem.at[slot], device)

    def await_answer(key):
        first, _, _, slot = links[key]

        @pl.when(first)
        def _():
            pl.semaphore_wait(ready_sem.at[slot], 1)

    class Gather:
        def __init__(self, shard, half=None):
            self.shard = shard
            self.half = half
            self.first = slots(16)
            self.second = slots(4)

        def start(self):
            for dz in (1, 3, 2):
                send(self.shard(0, 0), self.shard(0, 0), self.first + dz * 4, at(dz=dz))
            self.along_y(0)

        def along_y(self, dz):
            for dy in (1, 3) if self.half and dz in RELAYED else (1, 3, 2):
                send(self.shard(dz, 0), self.shard(dz, 0), self.first + dz * 4 + dy, at(dy=dy))

        def relay(self, dz):
            for side, dy, slot in ((0, 1, self.first + dz * 4 + 2), (1, 3, self.second + dz)):
                self.wait(dz, dy)
                part = self.half(side, dz, dy)
                send(part, part, slot, at(dy=dy))

        def wait_halves(self, dz):
            arrive(self.half(0, dz, 2), self.first + dz * 4 + 2)
            arrive(self.half(1, dz, 2), self.second + dz)

        def wait(self, dz, dy):
            arrive(self.shard(dz, dy), self.first + dz * 4 + dy)

    kv_gather = Gather(lambda dz, dy: kv_all.at[core, place_of(dz, dy)])
    kv_gather.start()
    sib_first = slots(16)

    def to_sibling(dz, dy):
        part = kv_gather.shard(dz, dy)
        send(part, part, sib_first + dz * 4 + dy, at(dk=1))

    act_first = slots(16)
    act_sib = slots(16)

    def act_shard(dzh, dx):
        index = ((zh - dzh) % 4) * 8 + ((x - dx) % 4) * 2 + core
        return act.at[pl.ds(pl.multiple_of(index * 64, 64), 64)]

    def act_from_sibling(dzh, dx):
        index = ((zh - dzh) % 4) * 8 + ((x - dx) % 4) * 2 + sib
        return act.at[pl.ds(pl.multiple_of(index * 64, 64), 64)]

    def act_along_x(dzh):
        for dx in (1, 3, 2):
            send(act_shard(dzh, 0), act_shard(dzh, 0), act_first + dzh * 4 + dx, at(dx=dx))
        act_to_sibling(dzh, 0)

    def act_to_sibling(dzh, dx):
        send(act_shard(dzh, dx), act_shard(dzh, dx), act_sib + dzh * 4 + dx, at(dk=1))

    act_z = {
        dzh: copy(act_shard(0, 0), act_shard(0, 0), act_first + dzh * 4, at(dzh=dzh))
        for dzh in (1, 3, 2)
    }
    sends.extend(act_z.values())

    for key in links:
        answer(key)
    def act_z_lower(to_first):
        for dzh in (1, 3, 2):
            first_rank = (zh + dzh) % 4 == 0
            chosen = first_rank if to_first else jnp.logical_not(first_rank)

            @pl.when(jnp.logical_not(links["z", dzh][0]) & chosen)
            def _(dzh=dzh):
                act_z[dzh].start()

    act_z_lower(True)

    def act_z_later(pairs):
        for dzh in (1, 3, 2):
            first, _, _, slot = links["z", dzh]
            farthest = (zh == 0) & (dzh == 2)

            @pl.when(first & (farthest if pairs == "far" else jnp.logical_not(farthest)))
            def _(dzh=dzh, slot=slot):
                pl.semaphore_wait(ready_sem.at[slot], 1)
                act_z[dzh].start()

    for item in loads[3:]:
        item.wait()
    row_ids = lax.broadcasted_iota(jnp.int32, (2 * SHARD, SHARD), 0) % SHARD + ctx * SHARD
    pick = (
        lax.broadcasted_iota(jnp.int32, (2 * SHARD, 32), 1)
        == (lax.broadcasted_iota(jnp.int32, (2 * SHARD, 32), 0) % SHARD + ctx * SHARD) // BLK
    )
    mask_rows = dot(pick.astype(BF16), mask_in[...].astype(BF16)).astype(BF16)

    def bias_step(step, carry):
        cols = pl.ds(pl.multiple_of(step * SHARD, SHARD), SHARD)
        first = ((step % 4) * 4 + step // 4) * SHARD
        col_ids = lax.broadcasted_iota(jnp.int32, (2 * SHARD, SHARD), 1) + first
        spread = (
            (lax.broadcasted_iota(jnp.int32, (32, SHARD), 1) + first) // BLK
            == lax.broadcasted_iota(jnp.int32, (32, SHARD), 0)
        )
        wide = dot(mask_rows, spread.astype(BF16))
        bias[:, cols] = jnp.where((wide > 0.5) & (col_ids <= row_ids), 0.0, NEG)
        return carry

    lax.fori_loop(0, TOK // SHARD, bias_step, 0, unroll=2)
    query = stacked(query_in[...])
    grad = stacked(grad_in[...])
    delta = jnp.sum(grad.astype(F32) * stacked(out_in[...]).astype(F32), axis=1, keepdims=True)

    def mine_first(value):
        turned = value.astype(F32).T
        low, high = turned[:64], turned[64:]
        return jnp.concatenate(
            [jnp.where(core == 0, low, high), jnp.where(core == 0, high, low)], axis=0
        )

    query_turned[...] = mine_first(query)
    grad_turned[...] = mine_first(grad)

    def block_scores(dz, dy):
        span = place_of(dz, dy)
        if dz or dy:
            arrive(kv_all.at[sib, span], sib_first + dz * 4 + dy)
        part = dot_t(query, kv_all[0, span, :]) + bias[:, span]
        scores[:, span] = part
        slopes[:, span] = dot_t(grad, kv_all[1, span, :])
        top[...] = jnp.maximum(top[...], part) if dz or dy else part

    block_scores(0, 0)

    for dz in (1, 3, 2):
        kv_gather.wait(dz, 0)
        kv_gather.along_y(dz)
        to_sibling(dz, 0)
    act_z_lower(False)
    for dx in (1, 3, 2):
        await_answer(("x", dx))
    act_along_x(0)

    waiting = [(1, 0), (3, 0), (2, 0)]
    for dz in (0, 1, 3, 2):
        for dy in (1, 3, 2):
            kv_gather.wait(dz, dy)
            to_sibling(dz, dy)
            waiting.append((dz, dy))
            if len(waiting) > 2:
                block_scores(*waiting.pop(0))
        if dz == 1:
            act_z_later("near")
    for block in waiting:
        block_scores(*block)

    act_z_later("far")
    scale = HD ** -0.5
    power = scale * 1.4426950408889634
    row_max = jnp.max(top[...], axis=1, keepdims=True)
    total = jnp.zeros((2 * SHARD, HD), F32)
    for step in range(TOK // SPAN):
        cols = slice(step * SPAN, (step + 1) * SPAN)
        part = jnp.exp2((scores[:, cols] - row_max) * power)
        scores[:, cols] = part
        probs[:, cols] = part.astype(BF16)
        for lane in range(0, SPAN, HD):
            total = total + part[:, lane : lane + HD]
    inverse_row = 1.0 / jnp.sum(total.T, axis=0, keepdims=True)
    query_t = (query_turned[...] * (inverse_row * scale)).astype(BF16)
    grad_t = (grad_turned[...] * inverse_row).astype(BF16)

    core_slot = slots(8)
    y_slot = slots(8)

    def span_of(dy):
        return pl.ds(pl.multiple_of(((y + dy) % 4) * SPAN, SPAN), SPAN)

    def terms(part, dy):
        span = span_of(dy)
        if part:
            result = dot(grad_t, probs[:, span])
        else:
            slope = (scores[:, span] * (slopes[:, span] - delta)).astype(BF16)
            dsc[:, span] = slope
            result = dot(query_t, slope)
        for step in range(4):
            lanes = slice(step * SHARD, (step + 1) * SHARD)
            own[part, dy, step] = result[:64, lanes]
            sib_send[part, dy, step] = result[64:, lanes].astype(BF16)
        send(sib_send.at[part, dy], sib_recv.at[part, dy], core_slot + part * 4 + dy, at(dk=1))

    def to_y(part, dy):
        arrive(sib_recv.at[part, dy], core_slot + part * 4 + dy)
        y_send[part, dy - 1] = (own[part, dy] + sib_recv[part, dy].astype(F32)).astype(BF16)
        send(
            y_send.at[part, dy - 1], y_recv.at[part, dy - 1], y_slot + part * 4 + dy, at(dy=dy)
        )

    for dy in (2, 1, 3, 0):
        terms(1, dy)
    terms(0, 2)
    to_y(1, 2)
    to_y(1, 1)
    terms(0, 1)
    to_y(1, 3)
    terms(0, 3)
    to_y(0, 2)
    terms(0, 0)
    to_y(0, 1)
    to_y(0, 3)

    inverse = 1.0 / jnp.sum(total, axis=1, keepdims=True)
    query_grad = dot(dsc[...], kv_all[0]) * (inverse * scale)
    q_out[:, :HD] = query_grad[:SHARD].astype(BF16)
    q_out[:, HD:] = query_grad[SHARD:].astype(BF16)
    own_lanes = pl.ds(pl.multiple_of(ctx * SHARD, SHARD), SHARD)
    q_all[:HD, own_lanes] = query_grad[:SHARD].T.astype(BF16)
    q_all[HD:, own_lanes] = query_grad[SHARD:].T.astype(BF16)

    def lanes_of(dz, dy):
        index = ((z - dz) % 4) * 4 + (y - dy) % 4
        return pl.ds(pl.multiple_of(index * SHARD, SHARD), SHARD)

    q_gather = Gather(
        lambda dz, dy: q_all.at[:, lanes_of(dz, dy)],
        lambda part, dz, dy: q_all.at[pl.ds(part * HD, HD), lanes_of(dz, dy)],
    )
    q_gather.start()

    for dzh in (1, 3):
        arrive(act_shard(dzh, 0), act_first + dzh * 4)
        act_along_x(dzh)

    zx_slot = slots(8)

    def to_zx(part):
        arrive(sib_recv.at[part, 0], core_slot + part * 4)
        for dy in (1, 3, 2):
            arrive(y_recv.at[part, dy - 1], y_slot + part * 4 + dy)
        y_sum = own[part, 0] + sib_recv[part, 0].astype(F32)
        for dy in (1, 2, 3):
            y_sum = y_sum + y_recv[part, dy - 1].astype(F32)
        own[part, 0] = y_sum
        zx_send[part] = y_sum.astype(BF16)
        other = jnp.where(side == part, 0, 1)
        for dz in (1, 3, 2):
            slot = dz * 2 + other
            target = (z + dz) % 4
            device = (target * 4 + y, zh * 8 + (x - side + part) * 2 + core)

            @pl.when(target < z)
            def _(target=target, slot=slot, device=device):
                copy(zx_send.at[part, target], zx_recv.at[slot], zx_slot + slot, device).start()

        @pl.when(side != part)
        def _():
            copy(zx_send.at[part, z], zx_recv.at[1], zx_slot + 1, flip(0)).start()

    for dz in (1, 2, 3):
        await_answer(("f", dz))
    to_zx(1)
    for dz in (1, 3):
        q_gather.wait(dz, 0)
        q_gather.along_y(dz)
    to_zx(0)
    sends.append(copy(zx_send.at[0, 0], zx_recv.at[1], zx_slot + 1, flip(0)))

    q_gather.wait(2, 0)
    q_gather.along_y(2)
    arrive(act_shard(2, 0), act_first + 8)
    act_along_x(2)

    arrive(zx_recv.at[1], zx_slot + 1)
    own[0, 1, 0] = own[side, 0, z] + zx_recv[1].astype(F32)
    for dz in (1, 3, 2):
        @pl.when((z - dz) % 4 > z)
        def _(dz=dz):
            for slot in (dz * 2, dz * 2 + 1):
                arrive(zx_recv.at[slot], zx_slot + slot)
                own[0, 1, 0] = own[0, 1, 0] + zx_recv[slot].astype(F32)

    kv_sum = own[0, 1, 0]
    g_all[:, own_lanes] = kv_sum.astype(BF16)
    g_gather = Gather(lambda dz, dy: g_all.at[:, lanes_of(dz, dy)])
    g_gather.start()
    kv_out[...] = kv_sum.astype(BF16)
    q_gather.relay(0)
    q_gather.relay(1)
    q_gather.relay(3)

    for dz in (1, 3, 2):
        g_gather.wait(dz, 0)
        g_gather.along_y(dz)

    for dzh in (0, 1, 3):
        for dx in (1, 3, 2):
            arrive(act_shard(dzh, dx), act_first + dzh * 4 + dx)
            act_to_sibling(dzh, dx)

    for dx in (1, 3, 2):
        arrive(act_shard(2, dx), act_first + 8 + dx)
        act_to_sibling(2, dx)
    for dz in range(4):
        if dz in RELAYED:
            q_gather.wait_halves(dz)
        else:
            for dy in (1, 3, 2):
                q_gather.wait(dz, dy)
    for dzh in range(4):
        for dx in range(4):
            arrive(act_from_sibling(dzh, dx), act_sib + dzh * 4 + dx)
    wq_out[...] = dot(q_all[...], act[...]).T.astype(BF16)

    for dz in range(4):
        for dy in (1, 3, 2):
            g_gather.wait(dz, dy)
    wkv_out[...] = dot(g_all[...], act[...]).astype(BF16)

    for item in sends:
        item.wait_send()
    for dz in (1, 2, 3):
        @pl.when((z + dz) % 4 < z)
        def _(dz=dz):
            for slot in (dz * 2, dz * 2 + 1):
                copy(zx_send.at[0, 0], zx_recv.at[slot], zx_slot + slot, at(dz=dz)).wait_send()


def deliver(*refs):
    sources, results, sem = refs[:4], refs[4:8], refs[8]
    items = [
        pltpu.make_async_copy(source, result, sem.at[index])
        for index, (source, result) in enumerate(zip(sources, results))
    ]
    for item in items:
        item.start()
    for item in items:
        item.wait()


def per_device(inputs, queries, keys, values, outputs, out_grad, block_mask):
    vmem = pl.BlockSpec(memory_space=pltpu.VMEM)
    anywhere = pl.BlockSpec(memory_space=pl.ANY)
    shapes = (
        jax.ShapeDtypeStruct((SHARD, 256), BF16),
        jax.ShapeDtypeStruct((64, SHARD), BF16),
        jax.ShapeDtypeStruct((512, 256), BF16),
        jax.ShapeDtypeStruct((64, 512), BF16),
    )
    results = pl.pallas_call(
        body,
        name="attention_backward",
        out_shape=tuple(pltpu.VMEM(shape.shape, shape.dtype) for shape in shapes),
        in_specs=[anywhere] * 7,
        out_specs=(vmem, vmem, vmem, vmem),
        scratch_shapes=[
            pltpu.VMEM((SHARD, 256), BF16),
            pltpu.VMEM((SHARD, 256), BF16),
            pltpu.VMEM((SHARD, 256), BF16),
            pltpu.VMEM((32, 32), jnp.int32),
            pltpu.VMEM((TOK, 512), BF16),
            pltpu.VMEM((2, TOK, HD), BF16),
            pltpu.VMEM((256, TOK), BF16),
            pltpu.VMEM((64, TOK), BF16),
            pltpu.VMEM((256, TOK), F32),
            pltpu.VMEM((256, TOK), F32),
            pltpu.VMEM((256, TOK), BF16),
            pltpu.VMEM((256, TOK), BF16),
            pltpu.VMEM((256, TOK), F32),
            pltpu.VMEM((256, HD), F32),
            pltpu.VMEM((HD, 256), F32),
            pltpu.VMEM((HD, 256), F32),
            pltpu.VMEM((2, 4, 4, 64, HD), BF16),
            pltpu.VMEM((2, 4, 4, 64, HD), BF16),
            pltpu.VMEM((2, 4, 4, 64, HD), F32),
            pltpu.VMEM((2, 3, 4, 64, HD), BF16),
            pltpu.VMEM((2, 3, 4, 64, HD), BF16),
            pltpu.VMEM((2, 4, 64, HD), BF16),
            pltpu.VMEM((8, 64, HD), BF16),
            pltpu.SemaphoreType.DMA((152,)),
            pltpu.SemaphoreType.DMA((152,)),
            pltpu.SemaphoreType.DMA((7,)),
            pltpu.SemaphoreType.REGULAR((12,)),
        ],
        compiler_params=pltpu.CompilerParams(
            collective_id=0, has_side_effects=True, vmem_limit_bytes=VMEM_LIMIT
        ),
        cost_estimate=pl.CostEstimate(
            flops=1_400_000_000, bytes_accessed=4 << 20, transcendentals=256 * TOK
        ),
    )(inputs, queries, keys, values, outputs, out_grad, block_mask)
    q_grad, kv_turned, weight_q, weight_kv_turned = pl.pallas_call(
        deliver,
        name="deliver",
        out_shape=shapes,
        in_specs=[vmem] * 4,
        out_specs=[anywhere] * 4,
        scratch_shapes=[pltpu.SemaphoreType.DMA((4,))],
        compiler_params=pltpu.CompilerParams(vmem_limit_bytes=4 << 20),
    )(*results)
    return q_grad, kv_turned.T, weight_q, weight_kv_turned.T


def solution(mesh):
    in_specs = (
        P("head", "ctx"),
        P("ctx", "head"),
        P("ctx", None),
        P("ctx", None),
        P("ctx", "head"),
        P("ctx", "head"),
        P(),
    )
    out_specs = (P("ctx", "head"), P("ctx", "head"), P("ctx", "head"), P("ctx", "head"))
    return jax.shard_map(
        per_device, mesh=mesh, in_specs=in_specs, out_specs=out_specs, check_vma=False
    )
```

```python
import functools

import jax
import jax.numpy as jnp
from jax import lax
from jax.experimental import pallas as pl
from jax.experimental.pallas import tpu as pltpu
from jax.sharding import PartitionSpec as P

HD = 128
BLK = 64
TOK = 2048
SHARD = 128
SPAN = 512
RELAYED = (0, 1, 3)
MESH = pl.DeviceIdType.MESH
NEG = -1e30
VMEM_LIMIT = 60 << 20
F32 = jnp.float32
BF16 = jnp.bfloat16

def dot(left, right):
    return lax.dot_general(left, right, (((1,), (0,)), ((), ())), preferred_element_type=F32)


def dot_t(left, right):
    return lax.dot_general(left, right, (((1,), (1,)), ((), ())), preferred_element_type=F32)


def stacked(value):
    return jnp.concatenate([value[:, :HD], value[:, HD:]], axis=0)


def body(
    inputs, queries, keys, values, outputs, out_grad, block_mask,
    q_out, kv_out, wq_out, wkv_out,
    query_in, grad_in, out_in, mask_in,
    act, kv_all, q_all, g_all, scores, slopes, probs, dsc, bias, top, query_turned, grad_turned,
    sib_send, sib_recv, own, y_send, y_recv, zx_send, zx_recv,
    send_sem, recv_sem, local_sem, ready_sem,
):
    ctx = lax.axis_index("ctx")
    head = lax.axis_index("head")
    z, y = ctx // 4, ctx % 4
    zh, x, core = head // 8, (head // 2) % 4, head % 2
    sib = 1 - core
    side = x % 2
    group = head // 4

    def at(dz=0, dy=0, dzh=0, dx=0, dk=0):
        return (
            ((z + dz) % 4) * 4 + (y + dy) % 4,
            ((zh + dzh) % 4) * 8 + ((x + dx) % 4) * 2 + (core + dk) % 2,
        )

    def flip(dz):
        return (((z + dz) % 4) * 4 + y, zh * 8 + (x + 1 - 2 * side) * 2 + core)

    counter = [0]
    sends = []

    def slots(count):
        first = counter[0]
        counter[0] += count
        return first

    def copy(src, dst, slot, device):
        return pltpu.make_async_remote_copy(
            src_ref=src, dst_ref=dst, send_sem=send_sem.at[slot], recv_sem=recv_sem.at[slot],
            device_id=device, device_id_type=MESH,
        )

    def send(src, dst, slot, device):
        item = copy(src, dst, slot, device)
        item.start()
        sends.append(item)

    def arrive(dst, slot):
        copy(dst, dst, slot, at(dk=1)).wait_recv()

    def signal(sem, device):
        pl.semaphore_signal(sem, inc=1, device_id=device, device_id_type=MESH)

    def place_of(dz, dy):
        return pl.ds(pl.multiple_of((((y - dy) % 4) * 4 + (z - dz) % 4) * SHARD, SHARD), SHARD)

    own_rows = place_of(0, 0)
    own_cols = pl.ds(pl.multiple_of(group * HD, HD), HD)
    own_act = pl.ds(pl.multiple_of(head * 64, 64), 64)
    loads = [
        pltpu.make_async_copy(keys.at[:, own_cols], kv_all.at[0, own_rows], local_sem.at[0]),
        pltpu.make_async_copy(values.at[:, own_cols], kv_all.at[1, own_rows], local_sem.at[1]),
        pltpu.make_async_copy(inputs, act.at[own_act], local_sem.at[2]),
        pltpu.make_async_copy(block_mask, mask_in, local_sem.at[3]),
        pltpu.make_async_copy(queries, query_in, local_sem.at[4]),
        pltpu.make_async_copy(out_grad, grad_in, local_sem.at[5]),
        pltpu.make_async_copy(outputs, out_in, local_sem.at[6]),
    ]
    for item in loads:
        item.start()

    def rank_of(index):
        return jnp.where(index < 2, index, 5 - index)

    barrier = pltpu.get_barrier_semaphore()
    for offset in (1, 2, 3):
        signal(barrier, at(dy=offset))
        signal(barrier, at(dz=offset))
    signal(barrier, at(dk=1))

    rank_z, rank_x = rank_of(zh), rank_of(x)
    pair_first = (x == 0) | (x == 3)
    links = {}
    for offset in (1, 2, 3):
        links["z", offset] = (
            rank_z < rank_of((zh + offset) % 4), at(dzh=offset), offset, 4 - offset
        )
        links["x", offset] = (
            rank_x < rank_of((x + offset) % 4), at(dx=offset), 4 + offset, 8 - offset
        )
        links["f", offset] = (pair_first, flip(offset), 8 + offset, 12 - offset)

    for first, device, _, _ in links.values():
        @pl.when(first)
        def _(device=device):
            signal(barrier, device)

    for item in loads[:3]:
        item.wait()
    pl.semaphore_wait(barrier, 7 + rank_z + rank_x + jnp.where(pair_first, 0, 3))

    def answer(key):
        first, device, slot, _ = links[key]

        @pl.when(jnp.logical_not(first))
        def _():
            signal(ready_sem.at[slot], device)

    def await_answer(key):
        first, _, _, slot = links[key]

        @pl.when(first)
        def _():
            pl.semaphore_wait(ready_sem.at[slot], 1)

    class Gather:
        def __init__(self, shard, half=None):
            self.shard = shard
            self.half = half
            self.first = slots(16)
            self.second = slots(4)

        def start(self):
            for dz in (1, 3, 2):
                send(self.shard(0, 0), self.shard(0, 0), self.first + dz * 4, at(dz=dz))
            self.along_y(0)

        def along_y(self, dz):
            for dy in (1, 3) if self.half and dz in RELAYED else (1, 3, 2):
                send(self.shard(dz, 0), self.shard(dz, 0), self.first + dz * 4 + dy, at(dy=dy))

        def relay(self, dz):
            for side, dy, slot in ((0, 1, self.first + dz * 4 + 2), (1, 3, self.second + dz)):
                self.wait(dz, dy)
                part = self.half(side, dz, dy)
                send(part, part, slot, at(dy=dy))

        def wait_halves(self, dz):
            arrive(self.half(0, dz, 2), self.first + dz * 4 + 2)
            arrive(self.half(1, dz, 2), self.second + dz)

        def wait(self, dz, dy):
            arrive(self.shard(dz, dy), self.first + dz * 4 + dy)

    kv_gather = Gather(lambda dz, dy: kv_all.at[core, place_of(dz, dy)])
    kv_gather.start()
    sib_first = slots(16)

    def to_sibling(dz, dy):
        part = kv_gather.shard(dz, dy)
        send(part, part, sib_first + dz * 4 + dy, at(dk=1))

    act_first = slots(16)
    act_sib = slots(16)

    def act_shard(dzh, dx):
        index = ((zh - dzh) % 4) * 8 + ((x - dx) % 4) * 2 + core
        return act.at[pl.ds(pl.multiple_of(index * 64, 64), 64)]

    def act_from_sibling(dzh, dx):
        index = ((zh - dzh) % 4) * 8 + ((x - dx) % 4) * 2 + sib
        return act.at[pl.ds(pl.multiple_of(index * 64, 64), 64)]

    def act_along_x(dzh):
        for dx in (1, 3, 2):
            send(act_shard(dzh, 0), act_shard(dzh, 0), act_first + dzh * 4 + dx, at(dx=dx))
        act_to_sibling(dzh, 0)

    def act_to_sibling(dzh, dx):
        send(act_shard(dzh, dx), act_shard(dzh, dx), act_sib + dzh * 4 + dx, at(dk=1))

    act_z = {
        dzh: copy(act_shard(0, 0), act_shard(0, 0), act_first + dzh * 4, at(dzh=dzh))
        for dzh in (1, 3, 2)
    }
    sends.extend(act_z.values())

    for key in links:
        answer(key)
    def act_z_lower(to_first):
        for dzh in (1, 3, 2):
            first_rank = (zh + dzh) % 4 == 0
            chosen = first_rank if to_first else jnp.logical_not(first_rank)

            @pl.when(jnp.logical_not(links["z", dzh][0]) & chosen)
            def _(dzh=dzh):
                act_z[dzh].start()

    act_z_lower(True)

    def act_z_later(pairs):
        for dzh in (1, 3, 2):
            first, _, _, slot = links["z", dzh]
            farthest = (zh == 0) & (dzh == 2)

            @pl.when(first & (farthest if pairs == "far" else jnp.logical_not(farthest)))
            def _(dzh=dzh, slot=slot):
                pl.semaphore_wait(ready_sem.at[slot], 1)
                act_z[dzh].start()

    for item in loads[3:]:
        item.wait()
    row_ids = lax.broadcasted_iota(jnp.int32, (2 * SHARD, SHARD), 0) % SHARD + ctx * SHARD
    pick = (
        lax.broadcasted_iota(jnp.int32, (2 * SHARD, 32), 1)
        == (lax.broadcasted_iota(jnp.int32, (2 * SHARD, 32), 0) % SHARD + ctx * SHARD) // BLK
    )
    mask_rows = dot(pick.astype(BF16), mask_in[...].astype(BF16)).astype(BF16)

    def bias_step(step, carry):
        cols = pl.ds(pl.multiple_of(step * SHARD, SHARD), SHARD)
        first = ((step % 4) * 4 + step // 4) * SHARD
        col_ids = lax.broadcasted_iota(jnp.int32, (2 * SHARD, SHARD), 1) + first
        spread = (
            (lax.broadcasted_iota(jnp.int32, (32, SHARD), 1) + first) // BLK
            == lax.broadcasted_iota(jnp.int32, (32, SHARD), 0)
        )
        wide = dot(mask_rows, spread.astype(BF16))
        bias[:, cols] = jnp.where((wide > 0.5) & (col_ids <= row_ids), 0.0, NEG)
        return carry

    lax.fori_loop(0, TOK // SHARD, bias_step, 0, unroll=2)
    query = stacked(query_in[...])
    grad = stacked(grad_in[...])
    delta = jnp.sum(grad.astype(F32) * stacked(out_in[...]).astype(F32), axis=1, keepdims=True)

    def mine_first(value):
        turned = value.astype(F32).T
        low, high = turned[:64], turned[64:]
        return jnp.concatenate(
            [jnp.where(core == 0, low, high), jnp.where(core == 0, high, low)], axis=0
        )

    query_turned[...] = mine_first(query)
    grad_turned[...] = mine_first(grad)

    def block_scores(dz, dy):
        span = place_of(dz, dy)
        if dz or dy:
            arrive(kv_all.at[sib, span], sib_first + dz * 4 + dy)
        part = dot_t(query, kv_all[0, span, :]) + bias[:, span]
        scores[:, span] = part
        slopes[:, span] = dot_t(grad, kv_all[1, span, :])
        top[...] = jnp.maximum(top[...], part) if dz or dy else part

    block_scores(0, 0)

    for dz in (1, 3, 2):
        kv_gather.wait(dz, 0)
        kv_gather.along_y(dz)
        to_sibling(dz, 0)
    act_z_lower(False)
    for dx in (1, 3, 2):
        await_answer(("x", dx))
    act_along_x(0)

    waiting = [(1, 0), (3, 0), (2, 0)]
    for dz in (0, 1, 3, 2):
        for dy in (1, 3, 2):
            kv_gather.wait(dz, dy)
            to_sibling(dz, dy)
            waiting.append((dz, dy))
            if len(waiting) > 2:
                block_scores(*waiting.pop(0))
        if dz == 1:
            act_z_later("near")
    for block in waiting:
        block_scores(*block)

    act_z_later("far")
    scale = HD ** -0.5
    power = scale * 1.4426950408889634
    row_max = jnp.max(top[...], axis=1, keepdims=True)
    total = jnp.zeros((2 * SHARD, HD), F32)
    for step in range(TOK // SPAN):
        cols = slice(step * SPAN, (step + 1) * SPAN)
        part = jnp.exp2((scores[:, cols] - row_max) * power)
        scores[:, cols] = part
        probs[:, cols] = part.astype(BF16)
        for lane in range(0, SPAN, HD):
            total = total + part[:, lane : lane + HD]
    inverse_row = 1.0 / jnp.sum(total.T, axis=0, keepdims=True)
    query_t = (query_turned[...] * (inverse_row * scale)).astype(BF16)
    grad_t = (grad_turned[...] * inverse_row).astype(BF16)

    core_slot = slots(8)
    y_slot = slots(8)

    def span_of(dy):
        return pl.ds(pl.multiple_of(((y + dy) % 4) * SPAN, SPAN), SPAN)

    def terms(part, dy):
        span = span_of(dy)
        if part:
            result = dot(grad_t, probs[:, span])
        else:
            slope = (scores[:, span] * (slopes[:, span] - delta)).astype(BF16)
            dsc[:, span] = slope
            result = dot(query_t, slope)
        for step in range(4):
            lanes = slice(step * SHARD, (step + 1) * SHARD)
            own[part, dy, step] = result[:64, lanes]
            sib_send[part, dy, step] = result[64:, lanes].astype(BF16)
        send(sib_send.at[part, dy], sib_recv.at[part, dy], core_slot + part * 4 + dy, at(dk=1))

    def to_y(part, dy):
        arrive(sib_recv.at[part, dy], core_slot + part * 4 + dy)
        y_send[part, dy - 1] = (own[part, dy] + sib_recv[part, dy].astype(F32)).astype(BF16)
        send(
            y_send.at[part, dy - 1], y_recv.at[part, dy - 1], y_slot + part * 4 + dy, at(dy=dy)
        )

    for dy in (2, 1, 3, 0):
        terms(1, dy)
    terms(0, 2)
    to_y(1, 2)
    to_y(1, 1)
    terms(0, 1)
    to_y(1, 3)
    terms(0, 3)
    to_y(0, 2)
    terms(0, 0)
    to_y(0, 1)
    to_y(0, 3)

    inverse = 1.0 / jnp.sum(total, axis=1, keepdims=True)
    query_grad = dot(dsc[...], kv_all[0]) * (inverse * scale)
    q_out[:, :HD] = query_grad[:SHARD].astype(BF16)
    q_out[:, HD:] = query_grad[SHARD:].astype(BF16)
    own_lanes = pl.ds(pl.multiple_of(ctx * SHARD, SHARD), SHARD)
    q_all[:HD, own_lanes] = query_grad[:SHARD].T.astype(BF16)
    q_all[HD:, own_lanes] = query_grad[SHARD:].T.astype(BF16)

    def lanes_of(dz, dy):
        index = ((z - dz) % 4) * 4 + (y - dy) % 4
        return pl.ds(pl.multiple_of(index * SHARD, SHARD), SHARD)

    q_gather = Gather(
        lambda dz, dy: q_all.at[:, lanes_of(dz, dy)],
        lambda part, dz, dy: q_all.at[pl.ds(part * HD, HD), lanes_of(dz, dy)],
    )
    q_gather.start()

    for dzh in (1, 3):
        arrive(act_shard(dzh, 0), act_first + dzh * 4)
        act_along_x(dzh)

    zx_slot = slots(8)

    def to_zx(part):
        arrive(sib_recv.at[part, 0], core_slot + part * 4)
        for dy in (1, 3, 2):
            arrive(y_recv.at[part, dy - 1], y_slot + part * 4 + dy)
        y_sum = own[part, 0] + sib_recv[part, 0].astype(F32)
        for dy in (1, 2, 3):
            y_sum = y_sum + y_recv[part, dy - 1].astype(F32)
        own[part, 0] = y_sum
        zx_send[part] = y_sum.astype(BF16)
        other = jnp.where(side == part, 0, 1)
        for dz in (1, 3, 2):
            slot = dz * 2 + other
            target = (z + dz) % 4
            device = (target * 4 + y, zh * 8 + (x - side + part) * 2 + core)

            @pl.when(target < z)
            def _(target=target, slot=slot, device=device):
                copy(zx_send.at[part, target], zx_recv.at[slot], zx_slot + slot, device).start()

        @pl.when(side != part)
        def _():
            copy(zx_send.at[part, z], zx_recv.at[1], zx_slot + 1, flip(0)).start()

    for dz in (1, 2, 3):
        await_answer(("f", dz))
    to_zx(1)
    for dz in (1, 3):
        q_gather.wait(dz, 0)
        q_gather.along_y(dz)
    to_zx(0)
    sends.append(copy(zx_send.at[0, 0], zx_recv.at[1], zx_slot + 1, flip(0)))

    q_gather.wait(2, 0)
    q_gather.along_y(2)
    arrive(act_shard(2, 0), act_first + 8)
    act_along_x(2)

    arrive(zx_recv.at[1], zx_slot + 1)
    own[0, 1, 0] = own[side, 0, z] + zx_recv[1].astype(F32)
    for dz in (1, 3, 2):
        @pl.when((z - dz) % 4 > z)
        def _(dz=dz):
            for slot in (dz * 2, dz * 2 + 1):
                arrive(zx_recv.at[slot], zx_slot + slot)
                own[0, 1, 0] = own[0, 1, 0] + zx_recv[slot].astype(F32)

    kv_sum = own[0, 1, 0]
    g_all[:, own_lanes] = kv_sum.astype(BF16)
    g_gather = Gather(lambda dz, dy: g_all.at[:, lanes_of(dz, dy)])
    g_gather.start()
    kv_out[...] = kv_sum.astype(BF16)
    q_gather.relay(0)
    q_gather.relay(1)
    q_gather.relay(3)

    for dz in (1, 3, 2):
        g_gather.wait(dz, 0)
        g_gather.along_y(dz)

    for dzh in (0, 1, 3):
        for dx in (1, 3, 2):
            arrive(act_shard(dzh, dx), act_first + dzh * 4 + dx)
            act_to_sibling(dzh, dx)

    for dx in (1, 3, 2):
        arrive(act_shard(2, dx), act_first + 8 + dx)
        act_to_sibling(2, dx)
    for dzh in range(4):
        for dx in range(4):
            arrive(act_from_sibling(dzh, dx), act_sib + dzh * 4 + dx)
    weight_q = jnp.zeros((256, 512), F32)
    for dz in (0, 1, 3, 2):
        if dz in RELAYED:
            q_gather.wait_halves(dz)
        else:
            for dy in (1, 3, 2):
                q_gather.wait(dz, dy)
        tokens = pl.ds(pl.multiple_of(((z - dz) % 4) * SPAN, SPAN), SPAN)
        weight_q = weight_q + dot(q_all[:, tokens], act[tokens, :])
    wq_out[...] = weight_q.T.astype(BF16)

    for dz in range(4):
        for dy in (1, 3, 2):
            g_gather.wait(dz, dy)
    wkv_out[...] = dot(g_all[...], act[...]).astype(BF16)

    for item in sends:
        item.wait_send()
    for dz in (1, 2, 3):
        @pl.when((z + dz) % 4 < z)
        def _(dz=dz):
            for slot in (dz * 2, dz * 2 + 1):
                copy(zx_send.at[0, 0], zx_recv.at[slot], zx_slot + slot, at(dz=dz)).wait_send()


def deliver(*refs):
    sources, results, sem = refs[:4], refs[4:8], refs[8]
    items = [
        pltpu.make_async_copy(source, result, sem.at[index])
        for index, (source, result) in enumerate(zip(sources, results))
    ]
    for item in items:
        item.start()
    for item in items:
        item.wait()


def per_device(inputs, queries, keys, values, outputs, out_grad, block_mask):
    vmem = pl.BlockSpec(memory_space=pltpu.VMEM)
    anywhere = pl.BlockSpec(memory_space=pl.ANY)
    shapes = (
        jax.ShapeDtypeStruct((SHARD, 256), BF16),
        jax.ShapeDtypeStruct((64, SHARD), BF16),
        jax.ShapeDtypeStruct((512, 256), BF16),
        jax.ShapeDtypeStruct((64, 512), BF16),
    )
    results = pl.pallas_call(
        body,
        name="attention_backward",
        out_shape=tuple(pltpu.VMEM(shape.shape, shape.dtype) for shape in shapes),
        in_specs=[anywhere] * 7,
        out_specs=(vmem, vmem, vmem, vmem),
        scratch_shapes=[
            pltpu.VMEM((SHARD, 256), BF16),
            pltpu.VMEM((SHARD, 256), BF16),
            pltpu.VMEM((SHARD, 256), BF16),
            pltpu.VMEM((32, 32), jnp.int32),
            pltpu.VMEM((TOK, 512), BF16),
            pltpu.VMEM((2, TOK, HD), BF16),
            pltpu.VMEM((256, TOK), BF16),
            pltpu.VMEM((64, TOK), BF16),
            pltpu.VMEM((256, TOK), F32),
            pltpu.VMEM((256, TOK), F32),
            pltpu.VMEM((256, TOK), BF16),
            pltpu.VMEM((256, TOK), BF16),
            pltpu.VMEM((256, TOK), F32),
            pltpu.VMEM((256, HD), F32),
            pltpu.VMEM((HD, 256), F32),
            pltpu.VMEM((HD, 256), F32),
            pltpu.VMEM((2, 4, 4, 64, HD), BF16),
            pltpu.VMEM((2, 4, 4, 64, HD), BF16),
            pltpu.VMEM((2, 4, 4, 64, HD), F32),
            pltpu.VMEM((2, 3, 4, 64, HD), BF16),
            pltpu.VMEM((2, 3, 4, 64, HD), BF16),
            pltpu.VMEM((2, 4, 64, HD), BF16),
            pltpu.VMEM((8, 64, HD), BF16),
            pltpu.SemaphoreType.DMA((152,)),
            pltpu.SemaphoreType.DMA((152,)),
            pltpu.SemaphoreType.DMA((7,)),
            pltpu.SemaphoreType.REGULAR((12,)),
        ],
        compiler_params=pltpu.CompilerParams(
            collective_id=0, has_side_effects=True, vmem_limit_bytes=VMEM_LIMIT
        ),
        cost_estimate=pl.CostEstimate(
            flops=1_400_000_000, bytes_accessed=4 << 20, transcendentals=256 * TOK
        ),
    )(inputs, queries, keys, values, outputs, out_grad, block_mask)
    q_grad, kv_turned, weight_q, weight_kv_turned = pl.pallas_call(
        deliver,
        name="deliver",
        out_shape=shapes,
        in_specs=[vmem] * 4,
        out_specs=[anywhere] * 4,
        scratch_shapes=[pltpu.SemaphoreType.DMA((4,))],
        compiler_params=pltpu.CompilerParams(vmem_limit_bytes=4 << 20),
    )(*results)
    return q_grad, kv_turned.T, weight_q, weight_kv_turned.T


def solution(mesh):
    in_specs = (
        P("head", "ctx"),
        P("ctx", "head"),
        P("ctx", None),
        P("ctx", None),
        P("ctx", "head"),
        P("ctx", "head"),
        P(),
    )
    out_specs = (P("ctx", "head"), P("ctx", "head"), P("ctx", "head"), P("ctx", "head"))
    return jax.shard_map(
        per_device, mesh=mesh, in_specs=in_specs, out_specs=out_specs, check_vma=False
    )
```
